32 devices in a mesh: ia: 8 (over z, core), ja: 4 (over y, x).
Axes of the slice: x: 2, y: 2, z: 4, core: 2. Of those that a mesh axis runs over, the one named last changes fastest.
Arguments:
- slab_rows: bfloat16 [256, 96, 128], P('ia', 'ja'), may hold values from -6 to 6
- column_rows: bfloat16 [64, 96, 128], P('ja', 'ia'), may hold values from -6 to 6
- pair_tile: bfloat16 [256, 64, 128], P('ia', 'ja'), may hold values from -6 to 6
- cotangent: bfloat16 [256, 64, 128], P('ia', 'ja'), may hold values from -6 to 6
- weights_left: bfloat16 [128, 256], replicated, may hold values from -0.5 to 0.5
- weights_right: bfloat16 [128, 256], replicated, may hold values from -0.5 to 0.5
- gate_weight: bfloat16 [128, 128], replicated, may hold values from -0.5 to 0.5
- out_weight: bfloat16 [128, 128], replicated, may hold values from -0.5 to 0.5
- input_gain: float32 [128], replicated, may hold values from 0.1 to 1.9
- input_bias: float32 [128], replicated, may hold values from -3 to 3
- update_gain: float32 [128], replicated, may hold values from 0.1 to 1.9
- update_bias: float32 [128], replicated, may hold values from -3 to 3
Outputs:
- update: bfloat16 [256, 64, 128], P('ia', 'ja')
- grad_slab: bfloat16 [256, 96, 128], P('ia', 'ja')
- grad_columns: bfloat16 [64, 96, 128], P('ja', 'ia')
- grad_tile: bfloat16 [256, 64, 128], P('ia', 'ja')
The draws below stay inside these ranges and needn't reach their ends.
All inputs are finite; a program needn't handle non-finite values.
Results may differ from the reference program's by a relative error of at most 0.018.
Values may be sent and summed in bfloat16 or wider, within the bound.
A program may use at most 128 MiB of HBM per device.

```python
import jax
import jax.numpy as jnp
from jax import lax

CZ = 128
CH = 128
I_DEV = 32
J_DEV = 16
SLAB = 256
COLS = 64
RES = 96
N_IA = 8
N_JA = 4


def level_of(own_key, extent, pieces, smallest, top_value):
    loudness = 1.0
    for axis_at, blocks in pieces:
        draws = jax.random.uniform(jax.random.fold_in(jax.random.fold_in(own_key, 6), axis_at), (blocks,), jnp.float32, smallest / len(pieces), top_value / len(pieces))
        loudness = loudness * jnp.repeat(jnp.exp(draws), extent[axis_at] // blocks).reshape((-1,) + (1,) * (len(extent) - 1 - axis_at))
    return loudness


def noise(own_key, extent, width, reach, shards=(), dtype=jnp.bfloat16):
    factor_of = level_of(own_key, extent, shards, -0.22, 0.18) if shards else 1.0
    result = jax.random.normal(own_key, extent, jnp.float32) * width * factor_of
    return jnp.minimum(jnp.maximum(result, -reach), reach).astype(dtype)


def setup_inputs(seed: int = 0) -> dict:
    streams_of = jax.random.split(jax.random.key(seed), 13)
    slab_rows = noise(streams_of[0], (SLAB, RES, CZ), 1.0, 6.0, ((0, 8), (1, 4)))
    column_rows = noise(streams_of[1], (COLS, RES, CZ), 1.0, 6.0, ((0, 4), (1, 8)))
    pair_tile = noise(streams_of[2], (SLAB, COLS, CZ), 1.0, 6.0, ((0, 8), (1, 4)))
    cotangent = noise(streams_of[3], (SLAB, COLS, CZ), 1.0, 6.0, ((0, 8), (1, 4)))
    weights_left = noise(streams_of[4], (CZ, 2 * CH), CZ ** -0.5, 0.5)
    weights_right = noise(streams_of[5], (CZ, 2 * CH), CZ ** -0.5, 0.5)
    gate_weight = noise(streams_of[6], (CZ, CZ), CZ ** -0.5, 0.5)
    out_weight = noise(streams_of[7], (CH, CZ), CH ** -0.5, 0.5)
    input_gain = jnp.clip(1.0 + 0.18 * jax.random.normal(streams_of[8], (CZ,), jnp.float32), 0.1, 1.9)
    input_bias = noise(streams_of[9], (CZ,), 0.5, 3.0, (), jnp.float32)
    update_gain = jnp.clip(1.0 + 0.18 * jax.random.normal(streams_of[10], (CH,), jnp.float32), 0.1, 1.9)
    update_bias = noise(streams_of[11], (CH,), 0.5, 3.0, (), jnp.float32)
    return {"slab_rows": slab_rows, "column_rows": column_rows, "pair_tile": pair_tile, "cotangent": cotangent, "weights_left": weights_left, "weights_right": weights_right, "gate_weight": gate_weight, "out_weight": out_weight, "input_gain": input_gain, "input_bias": input_bias, "update_gain": update_gain, "update_bias": update_bias}


epsilon = 1e-05

def normalize(values, gain, bias):
    values = values.astype(jnp.float32)
    centre = lax.optimization_barrier(jnp.mean(values, axis=-1, keepdims=True))
    shifted = values - centre
    inverse = lax.rsqrt(lax.optimization_barrier(jnp.mean(shifted * shifted, axis=-1, keepdims=True)) + epsilon)
    scaled = shifted * inverse
    return (scaled * gain + bias, scaled, inverse)

def norm_back(scaled, inverse, grad_out, gain):
    grad_hat = grad_out * gain
    first_mean = lax.optimization_barrier(jnp.mean(grad_hat, axis=-1, keepdims=True))
    second_mean = lax.optimization_barrier(jnp.mean(grad_hat * scaled, axis=-1, keepdims=True))
    return inverse * (grad_hat - first_mean - scaled * second_mean)

def project(rows, weights, input_gain, input_bias):
    normed, scaled, inverse = normalize(rows, input_gain, input_bias)
    hidden = jnp.dot(normed.astype(jnp.bfloat16), weights, preferred_element_type=jnp.float32)
    half_width = weights.shape[1] // 2
    linear = hidden[..., :half_width]
    sigma = jax.nn.sigmoid(hidden[..., half_width:])
    return ((sigma * linear).astype(jnp.bfloat16), linear, sigma, scaled, inverse)

def project_back(grad_edge, linear, sigma, scaled, inverse, weights, input_gain):
    joined = jnp.concatenate([grad_edge * sigma, grad_edge * linear * sigma * (1.0 - sigma)], axis=-1)
    grad_norm = jnp.dot(joined.astype(jnp.bfloat16), weights.T, preferred_element_type=jnp.float32)
    return norm_back(scaled, inverse, grad_norm, input_gain).astype(jnp.bfloat16)

def reference(slab_rows, column_rows, pair_tile, cotangent, weights_left, weights_right, gate_weight, out_weight, input_gain, input_bias, update_gain, update_bias):
    left, lin_left, sig_left, scaled_left, inv_left = project(slab_rows, weights_left, input_gain, input_bias)
    right, lin_right, sig_right, scaled_right, inv_right = project(column_rows, weights_right, input_gain, input_bias)
    triangle = jnp.einsum('ikc,jkc->ijc', left.astype(jnp.float32), right.astype(jnp.float32))
    tri_norm, tri_scaled, tri_inverse = normalize(triangle, update_gain, update_bias)
    outer = jnp.dot(tri_norm.astype(jnp.bfloat16), out_weight, preferred_element_type=jnp.float32)
    tile_norm, tile_scaled, tile_inverse = normalize(pair_tile, input_gain, input_bias)
    gate_linear = jnp.dot(tile_norm.astype(jnp.bfloat16), gate_weight, preferred_element_type=jnp.float32)
    gate = jax.nn.sigmoid(gate_linear)
    update = (gate * outer).astype(jnp.bfloat16)
    grad_update = cotangent.astype(jnp.float32)
    grad_outer = (grad_update * gate).astype(jnp.bfloat16)
    grad_gate = (grad_update * outer * gate * (1.0 - gate)).astype(jnp.bfloat16)
    grad_tnorm = jnp.dot(grad_outer, out_weight.T, preferred_element_type=jnp.float32)
    grad_tri = norm_back(tri_scaled, tri_inverse, grad_tnorm, update_gain).astype(jnp.bfloat16)
    grad_pnorm = jnp.dot(grad_gate, gate_weight.T, preferred_element_type=jnp.float32)
    grad_tile = norm_back(tile_scaled, tile_inverse, grad_pnorm, input_gain).astype(jnp.bfloat16)
    slab_count = left.shape[0]
    col_count = right.shape[0]
    res_count = left.shape[1]
    hidden_count = left.shape[2]
    tri_by_cols = jnp.transpose(grad_tri.reshape(slab_count, N_JA, J_DEV, hidden_count), (1, 0, 2, 3))
    right_blocks = right.reshape(N_JA, J_DEV, res_count, hidden_count)

    def add_left(running, blocks):
        tri_block, right_block = blocks
        partial_sum = jnp.einsum('ijc,jkc->ikc', tri_block.astype(jnp.float32), right_block.astype(jnp.float32))
        rounded = lax.optimization_barrier(partial_sum.astype(jnp.bfloat16))
        return (running + rounded.astype(jnp.float32), None)
    grad_left, unused_left = lax.scan(add_left, jnp.zeros((slab_count, res_count, hidden_count), jnp.float32), (tri_by_cols, right_blocks))
    tri_by_rows = grad_tri.reshape(N_IA, I_DEV, col_count, hidden_count)
    left_blocks = left.reshape(N_IA, I_DEV, res_count, hidden_count)

    def add_right(running, blocks):
        tri_block, left_block = blocks
        partial_sum = jnp.einsum('ijc,ikc->jkc', tri_block.astype(jnp.float32), left_block.astype(jnp.float32))
        rounded = lax.optimization_barrier(partial_sum.astype(jnp.bfloat16))
        return (running + rounded.astype(jnp.float32), None)
    grad_right, unused_right = lax.scan(add_right, jnp.zeros((col_count, res_count, hidden_count), jnp.float32), (tri_by_rows, left_blocks))
    grad_slab = project_back(grad_left, lin_left, sig_left, scaled_left, inv_left, weights_left, input_gain)
    grad_columns = project_back(grad_right, lin_right, sig_right, scaled_right, inv_right, weights_right, input_gain)
    return (update, grad_slab, grad_columns, grad_tile)
```

```python
import functools
import math

import jax
import jax.numpy as jnp
from jax import lax
from jax.experimental import pallas as pl
from jax.experimental.pallas import tpu as pltpu
from jax.sharding import PartitionSpec as P

EPSILON = 1e-05
MESH = pl.DeviceIdType.MESH
F32 = jnp.float32
BF16 = jnp.bfloat16


def chunk_of(count, rows, most):
    return max(d for d in range(1, count + 1) if count % d == 0 and (d * rows <= most or d == 1))


def normalize(values):
    centre = jnp.mean(values, axis=-1, keepdims=True)
    shifted = values - centre
    inverse = lax.rsqrt(jnp.mean(shifted * shifted, axis=-1, keepdims=True) + EPSILON)
    return shifted * inverse, inverse


def norm_back(scaled, inverse, grad_out, gain):
    grad_hat = grad_out * gain
    first_mean = jnp.mean(grad_hat, axis=-1, keepdims=True)
    second_mean = jnp.mean(grad_hat * scaled, axis=-1, keepdims=True)
    return inverse * (grad_hat - first_mean - scaled * second_mean)


def dot(a, b):
    return jnp.dot(a, b, preferred_element_type=F32)


def dot_t(a, b):
    return lax.dot_general(a, b, (((1,), (1,)), ((), ())), preferred_element_type=F32)


def kernel(
    n_ia,
    n_ja,
    slab_ref,
    cols_ref,
    tile_ref,
    cot_ref,
    wl_ref,
    wr_ref,
    wg_ref,
    wo_ref,
    gain_ref,
    bias_ref,
    ugain_ref,
    ubias_ref,
    update_ref,
    gslab_ref,
    gcols_ref,
    gtile_ref,
    xs_l,
    xs_r,
    save_l,
    save_r,
    left_all,
    right_all,
    left_f,
    right_f,
    dl_recv,
    dr_recv,
    tri_t,
    dtri,
    save_t,
    lsend,
    lrecv,
    rsend,
    rrecv,
    dlsend,
    dlrecv,
    drsend,
    drrecv,
):
    my_ia, my_ja = lax.axis_index("ia"), lax.axis_index("ja")
    rows_i, k_l, ch = slab_ref.shape
    rows_j, k_r, _ = cols_ref.shape
    res = k_l * n_ja

    def ja_peer(s):
        return lax.rem(my_ja + s, n_ja)

    def ia_peer(s):
        return lax.rem(my_ia + s, n_ia)

    barrier = pltpu.get_barrier_semaphore()

    def greet_ja(s, c):
        pl.semaphore_signal(barrier, inc=1, device_id=(my_ia, ja_peer(s)), device_id_type=MESH)
        return c

    def greet_ia(s, c):
        pl.semaphore_signal(barrier, inc=1, device_id=(ia_peer(s), my_ja), device_id_type=MESH)
        return c

    lax.fori_loop(1, n_ja, greet_ja, 0)
    lax.fori_loop(1, n_ia, greet_ia, 0)

    gain = gain_ref[...]
    bias = bias_ref[...]
    ugain = ugain_ref[...]
    ubias = ubias_ref[...]

    def project(x_ref, xs, w_ref, save, edges, base):
        rows, count, _ = x_ref.shape
        pitch = xs.shape[0] // rows

        def widen(r, c):
            xs[pl.ds(pl.multiple_of(r * pitch, 8), count), :] = x_ref[r].astype(F32)
            return c

        lax.fori_loop(0, rows, widen, 0, unroll=4)
        step = chunk_of(count, rows, 256)

        def body(t, c):
            k0 = t * step
            x = jnp.concatenate(
                [xs[pl.ds(k0 + u, rows, stride=pitch), :] for u in range(step)], axis=0
            )
            scaled, inverse = normalize(x)
            q = dot((scaled * gain + bias).astype(BF16), w_ref[...])
            linear = q[:, :ch]
            sigma = jax.nn.sigmoid(q[:, ch:])
            at = pl.ds(pl.multiple_of(k0 * rows, 8), step * rows)
            save[0, at, :] = scaled
            save[1, at, :] = jnp.broadcast_to(inverse, scaled.shape)
            save[2, at, :] = linear
            save[3, at, :] = sigma
            edge = (sigma * linear).astype(BF16)
            edges[pl.ds(base + k0, step)] = edge.reshape(step, rows, ch)
            return c

        lax.fori_loop(0, count // step, body, 0)

    def left_copy(s):
        own = left_all.at[pl.ds(my_ja * k_l, k_l)]
        return pltpu.make_async_remote_copy(
            src_ref=own,
            dst_ref=own,
            send_sem=lsend.at[s],
            recv_sem=lrecv.at[s],
            device_id=(my_ia, ja_peer(s)),
            device_id_type=MESH,
        )

    def right_copy(s):
        own = right_all.at[pl.ds(my_ia * k_r, k_r)]
        return pltpu.make_async_remote_copy(
            src_ref=own,
            dst_ref=own,
            send_sem=rsend.at[s],
            recv_sem=rrecv.at[s],
            device_id=(ia_peer(s), my_ja),
            device_id_type=MESH,
        )

    def dl_copy(s):
        to = ja_peer(s)
        return pltpu.make_async_remote_copy(
            src_ref=left_all.at[pl.ds(to * k_l, k_l)],
            dst_ref=dl_recv.at[s],
            send_sem=dlsend.at[s],
            recv_sem=dlrecv.at[s],
            device_id=(my_ia, to),
            device_id_type=MESH,
        )

    def dr_copy(s):
        to = ia_peer(s)
        return pltpu.make_async_remote_copy(
            src_ref=right_all.at[pl.ds(to * k_r, k_r)],
            dst_ref=dr_recv.at[s],
            send_sem=drsend.at[s],
            recv_sem=drrecv.at[s],
            device_id=(to, my_ja),
            device_id_type=MESH,
        )

    def each(copy, n, act):
        def body(s, c):
            act(copy(s))
            return c

        lax.fori_loop(1, n, body, 0)

    project(cols_ref, xs_r, wr_ref, save_r, right_all, my_ia * k_r)
    pl.semaphore_wait(barrier, n_ia + n_ja - 2)
    each(right_copy, n_ia, lambda c: c.start())
    project(slab_ref, xs_l, wl_ref, save_l, left_all, my_ja * k_l)
    each(left_copy, n_ja, lambda c: c.start())

    t_rows = chunk_of(rows_i, rows_j, 128)
    t_flat = t_rows * rows_j

    def tile_slot(t):
        return pl.ds(pl.multiple_of(t * t_flat, 8), t_flat)

    def gate_body(t, c):
        x = tile_ref[pl.ds(t * t_rows, t_rows)].astype(F32).reshape(t_flat, ch)
        scaled, inverse = normalize(x)
        gate = jax.nn.sigmoid(dot((scaled * gain + bias).astype(BF16), wg_ref[...]))
        at = tile_slot(t)
        save_t[0, at, :] = scaled
        save_t[1, at, :] = jnp.broadcast_to(inverse, scaled.shape)
        save_t[2, at, :] = gate
        return c

    lax.fori_loop(0, rows_i // t_rows, gate_body, 0)

    each(right_copy, n_ia, lambda c: c.wait())
    each(left_copy, n_ja, lambda c: c.wait())

    def to_f32(k, c):
        left_f[k] = left_all[k].astype(F32)
        right_f[k] = right_all[k].astype(F32)
        return c

    lax.fori_loop(0, res, to_f32, 0, unroll=4)

    block = math.gcd(rows_j, 8)
    for first in range(0, rows_j, block):

        def tri_body(k, accs, first=first):
            l = left_f[k]
            return tuple(
                acc + right_f[k, pl.ds(first + j, 1), :] * l for j, acc in enumerate(accs)
            )

        accs = lax.fori_loop(
            0, res, tri_body, tuple(jnp.zeros((rows_i, ch), F32) for _ in range(block)), unroll=2
        )
        for j, acc in enumerate(accs):
            tri_t[pl.ds((first + j) * rows_i, rows_i), :] = acc

    def tile_body(t, c):
        at = tile_slot(t)
        tri = jnp.concatenate(
            [tri_t[pl.ds(t * t_rows + u, rows_j, stride=rows_i), :] for u in range(t_rows)], axis=0
        )
        scaled, inverse = normalize(tri)
        outer = dot((scaled * ugain + ubias).astype(BF16), wo_ref[...])
        gate = save_t[2, at, :]
        update_ref[pl.ds(t * t_rows, t_rows)] = (
            (gate * outer).astype(BF16).reshape(t_rows, rows_j, ch)
        )
        cot = cot_ref[pl.ds(t * t_rows, t_rows)].astype(F32).reshape(t_flat, ch)
        d_outer = (cot * gate).astype(BF16)
        save_t[3, at, :] = cot * outer * gate * (1.0 - gate)
        d_tri = norm_back(scaled, inverse, dot_t(d_outer, wo_ref[...]), ugain)
        d_tri = d_tri.astype(BF16).astype(F32)
        dtri[at, :] = d_tri
        for u in range(t_rows):
            tri_t[pl.ds(t * t_rows + u, rows_j, stride=rows_i), :] = d_tri[
                u * rows_j : (u + 1) * rows_j
            ]
        return c

    lax.fori_loop(0, rows_i // t_rows, tile_body, 0)

    def left_part(s):
        k_first = ja_peer(s) * k_l
        u_l = math.gcd(k_l, 4)

        def body(t, c):
            k0 = k_first + t * u_l
            accs = [None] * u_l
            for j in range(rows_j):
                d = tri_t[pl.ds(j * rows_i, rows_i), :]
                for u in range(u_l):
                    term = right_f[k0 + u, pl.ds(j, 1), :] * d
                    accs[u] = term if j == 0 else accs[u] + term
            for u in range(u_l):
                left_all[k0 + u] = accs[u].astype(BF16)
            return c

        lax.fori_loop(0, k_l // u_l, body, 0)

    def right_part(s):
        k_first = ia_peer(s) * k_r
        u_r = math.gcd(k_r, 4)

        def body(t, c):
            k0 = k_first + t * u_r
            accs = [None] * u_r
            for i in range(rows_i):
                d = dtri[pl.ds(i * rows_j, rows_j), :]
                for u in range(u_r):
                    term = left_f[k0 + u, pl.ds(i, 1), :] * d
                    accs[u] = term if i == 0 else accs[u] + term
            for u in range(u_r):
                right_all[k0 + u] = accs[u].astype(BF16)
            return c

        lax.fori_loop(0, k_r // u_r, body, 0)

    groups = min(n_ia, n_ja)

    def group_body(g, c):
        def one_right(v, c):
            s = g * (n_ia // groups) + v + 1
            right_part(s)

            @pl.when(s < n_ia)
            def _():
                dr_copy(s).start()

            return c

        def one_left(v, c):
            s = g * (n_ja // groups) + v + 1
            left_part(s)

            @pl.when(s < n_ja)
            def _():
                dl_copy(s).start()

            return c

        lax.fori_loop(0, n_ia // groups, one_right, 0)
        lax.fori_loop(0, n_ja // groups, one_left, 0)
        return c

    lax.fori_loop(0, groups, group_body, 0)

    def tile_back(t, c):
        at = tile_slot(t)
        grad = dot_t(save_t[3, at, :].astype(BF16), wg_ref[...])
        out = norm_back(save_t[0, at, :], save_t[1, at, :], grad, gain)
        gtile_ref[pl.ds(t * t_rows, t_rows)] = out.astype(BF16).reshape(t_rows, rows_j, ch)
        return c

    lax.fori_loop(0, rows_i // t_rows, tile_back, 0)

    def project_back(out_ref, xs, w_ref, save, edges, base, recv, n):
        rows, count, _ = out_ref.shape
        pitch = xs.shape[0] // rows
        step = chunk_of(count, rows, 256)

        def body(t, c):
            k0 = t * step
            at = pl.ds(pl.multiple_of(k0 * rows, 8), step * rows)
            d = edges[pl.ds(base + k0, step)].astype(F32)

            def add(s, d):
                return d + recv[s, pl.ds(k0, step)].astype(F32)

            d = lax.fori_loop(1, n, add, d, unroll=n <= 8).reshape(step * rows, ch)
            linear, sigma = save[2, at, :], save[3, at, :]
            p = jnp.concatenate([d * sigma, d * linear * sigma * (1.0 - sigma)], axis=-1)
            grad = dot_t(p.astype(BF16), w_ref[...])
            out = norm_back(save[0, at, :], save[1, at, :], grad, gain)
            for u in range(step):
                xs[pl.ds(k0 + u, rows, stride=pitch), :] = out[u * rows : (u + 1) * rows]
            return c

        lax.fori_loop(0, count // step, body, 0)

        def narrow(r, c):
            out_ref[r] = xs[pl.ds(pl.multiple_of(r * pitch, 8), count), :].astype(BF16)
            return c

        lax.fori_loop(0, rows, narrow, 0, unroll=4)

    each(dr_copy, n_ia, lambda c: c.wait())
    project_back(gcols_ref, xs_r, wr_ref, save_r, right_all, my_ia * k_r, dr_recv, n_ia)
    each(dl_copy, n_ja, lambda c: c.wait())
    project_back(gslab_ref, xs_l, wl_ref, save_l, left_all, my_ja * k_l, dl_recv, n_ja)


def solution(mesh):
    n_ia, n_ja = mesh.shape["ia"], mesh.shape["ja"]

    def shards(slab, cols, tile, cot, wl, wr, wg, wo, gain, bias, ugain, ubias):
        rows_i, k_l, ch = slab.shape
        rows_j, k_r, _ = cols.shape
        res = k_l * n_ja
        pad_l, pad_r = -(-k_l // 8) * 8, -(-k_r // 8) * 8
        vmem = pl.BlockSpec(memory_space=pltpu.VMEM)
        flat = rows_i * rows_j
        dma = pltpu.SemaphoreType.DMA
        return pl.pallas_call(
            functools.partial(kernel, n_ia, n_ja),
            out_shape=[jax.ShapeDtypeStruct(a.shape, BF16) for a in (tile, slab, cols, tile)],
            in_specs=[vmem] * 12,
            out_specs=[vmem] * 4,
            scratch_shapes=[
                pltpu.VMEM((rows_i * pad_l, ch), F32),
                pltpu.VMEM((rows_j * pad_r, ch), F32),
                pltpu.VMEM((4, rows_i * k_l, ch), F32),
                pltpu.VMEM((4, rows_j * k_r, ch), F32),
                pltpu.VMEM((res, rows_i, ch), BF16),
                pltpu.VMEM((res, rows_j, ch), BF16),
                pltpu.VMEM((res, rows_i, ch), F32),
                pltpu.VMEM((res, rows_j, ch), F32),
                pltpu.VMEM((n_ja, k_l, rows_i, ch), BF16),
                pltpu.VMEM((n_ia, k_r, rows_j, ch), BF16),
                pltpu.VMEM((flat, ch), F32),
                pltpu.VMEM((flat, ch), F32),
                pltpu.VMEM((4, flat, ch), F32),
            ]
            + [dma((n,)) for n in (n_ja, n_ja, n_ia, n_ia, n_ja, n_ja, n_ia, n_ia)],
            compiler_params=pltpu.CompilerParams(
                collective_id=0, has_side_effects=True, vmem_limit_bytes=56 * 1024 * 1024
            ),
        )(
            slab, cols, tile, cot, wl, wr, wg, wo,
            gain[None, :], bias[None, :], ugain[None, :], ubias[None, :],
        )

    return jax.shard_map(
        shards,
        mesh=mesh,
        in_specs=(
            P("ia", "ja", None),
            P("ja", "ia", None),
            P("ia", "ja", None),
            P("ia", "ja", None),
        )
        + (P(),) * 8,
        out_specs=(
            P("ia", "ja", None),
            P("ia", "ja", None),
            P("ja", "ia", None),
            P("ia", "ja", None),
        ),
        check_vma=False,
    )
```

```python
import functools
import math

import jax
import jax.numpy as jnp
from jax import lax
from jax.experimental import pallas as pl
from jax.experimental.pallas import tpu as pltpu
from jax.sharding import PartitionSpec as P

EPSILON = 1e-05
MESH = pl.DeviceIdType.MESH
F32 = jnp.float32
BF16 = jnp.bfloat16


def chunk_of(count, rows, most):
    return max(d for d in range(1, count + 1) if count % d == 0 and (d * rows <= most or d == 1))


def normalize(values):
    centre = jnp.mean(values, axis=-1, keepdims=True)
    shifted = values - centre
    inverse = lax.rsqrt(jnp.mean(shifted * shifted, axis=-1, keepdims=True) + EPSILON)
    return shifted * inverse, inverse


def norm_back(scaled, inverse, grad_out, gain):
    grad_hat = grad_out * gain
    first_mean = jnp.mean(grad_hat, axis=-1, keepdims=True)
    second_mean = jnp.mean(grad_hat * scaled, axis=-1, keepdims=True)
    return inverse * (grad_hat - first_mean - scaled * second_mean)


def dot(a, b):
    return jnp.dot(a, b, preferred_element_type=F32)


def dot_t(a, b):
    return lax.dot_general(a, b, (((1,), (1,)), ((), ())), preferred_element_type=F32)


def kernel(
    n_ia,
    n_ja,
    slab_hbm,
    cols_hbm,
    tile_hbm,
    cot_hbm,
    wl_hbm,
    wr_hbm,
    wg_hbm,
    wo_hbm,
    gain_hbm,
    bias_hbm,
    ugain_hbm,
    ubias_hbm,
    update_hbm,
    gslab_hbm,
    gcols_hbm,
    gtile_hbm,
    slab_ref,
    cols_ref,
    tile_ref,
    cot_ref,
    wl_ref,
    wr_ref,
    wg_ref,
    wo_ref,
    gain_ref,
    bias_ref,
    ugain_ref,
    ubias_ref,
    update_ref,
    gslab_ref,
    gcols_ref,
    gtile_ref,
    in_sem,
    out_sem,
    xs_l,
    save_l,
    save_r,
    left_all,
    right_all,
    left_f,
    right_f,
    dl_recv,
    dr_recv,
    tri_t,
    dtri,
    save_t,
    lsend,
    lrecv,
    rsend,
    rrecv,
    dlsend,
    dlrecv,
    drsend,
    drrecv,
):
    my_ia, my_ja = lax.axis_index("ia"), lax.axis_index("ja")
    rows_i, k_l, ch = slab_ref.shape
    k_r, rows_j, _ = cols_ref.shape

    ins = [
        pltpu.make_async_copy(a, b, in_sem.at[n])
        for n, (a, b) in enumerate(
            [
                (cols_hbm, cols_ref),
                (wr_hbm, wr_ref),
                (gain_hbm, gain_ref),
                (bias_hbm, bias_ref),
                (slab_hbm, slab_ref),
                (wl_hbm, wl_ref),
                (tile_hbm, tile_ref),
                (wg_hbm, wg_ref),
                (cot_hbm, cot_ref),
                (wo_hbm, wo_ref),
                (ugain_hbm, ugain_ref),
                (ubias_hbm, ubias_ref),
            ]
        )
    ]
    outs = [
        pltpu.make_async_copy(a, b, out_sem.at[n])
        for n, (a, b) in enumerate(
            [
                (update_ref, update_hbm),
                (gtile_ref, gtile_hbm),
                (gcols_ref, gcols_hbm),
                (gslab_ref, gslab_hbm),
            ]
        )
    ]
    for copy in ins:
        copy.start()

    def ja_peer(s):
        return lax.rem(my_ja + s, n_ja)

    def ia_peer(s):
        return lax.rem(my_ia + s, n_ia)

    barrier = pltpu.get_barrier_semaphore()

    def greet_ja(s, c):
        pl.semaphore_signal(barrier, inc=1, device_id=(my_ia, ja_peer(s)), device_id_type=MESH)
        return c

    def greet_ia(s, c):
        pl.semaphore_signal(barrier, inc=1, device_id=(ia_peer(s), my_ja), device_id_type=MESH)
        return c

    lax.fori_loop(1, n_ja, greet_ja, 0)
    lax.fori_loop(1, n_ia, greet_ia, 0)

    for copy in ins[:4]:
        copy.wait()
    gain = gain_ref[...]
    bias = bias_ref[...]
    pitch = xs_l.shape[0] // rows_i

    def slab_piece(k0, step):
        return jnp.concatenate(
            [xs_l[pl.ds(k0 + u, rows_i, stride=pitch), :] for u in range(step)], axis=0
        )

    def cols_piece(k0, step):
        return cols_ref[pl.ds(k0, step)].astype(F32).reshape(step * rows_j, ch)

    def project(piece, rows, count, w_ref, save, edges, base):
        step = chunk_of(count, rows, 256)

        def body(t, c):
            k0 = t * step
            x = piece(k0, step)
            scaled, inverse = normalize(x)
            q = dot((scaled * gain + bias).astype(BF16), w_ref[...])
            linear = q[:, :ch]
            sigma = jax.nn.sigmoid(q[:, ch:])
            at = pl.ds(pl.multiple_of(k0 * rows, 8), step * rows)
            save[0, at, :] = scaled
            save[1, at, :] = jnp.broadcast_to(inverse, scaled.shape)
            save[2, at, :] = linear
            save[3, at, :] = sigma
            edge = (sigma * linear).astype(BF16)
            edges[pl.ds(base + k0, step)] = edge.reshape(step, rows, ch)
            return c

        lax.fori_loop(0, count // step, body, 0)

    def left_copy(s):
        own = left_all.at[pl.ds(my_ja * k_l, k_l)]
        return pltpu.make_async_remote_copy(
            src_ref=own,
            dst_ref=own,
            send_sem=lsend.at[s],
            recv_sem=lrecv.at[s],
            device_id=(my_ia, ja_peer(s)),
            device_id_type=MESH,
        )

    def right_copy(s):
        own = right_all.at[pl.ds(my_ia * k_r, k_r)]
        return pltpu.make_async_remote_copy(
            src_ref=own,
            dst_ref=own,
            send_sem=rsend.at[s],
            recv_sem=rrecv.at[s],
            device_id=(ia_peer(s), my_ja),
            device_id_type=MESH,
        )

    def dl_copy(s):
        to = ja_peer(s)
        return pltpu.make_async_remote_copy(
            src_ref=left_all.at[pl.ds(to * k_l, k_l)],
            dst_ref=dl_recv.at[s],
            send_sem=dlsend.at[s],
            recv_sem=dlrecv.at[s],
            device_id=(my_ia, to),
            device_id_type=MESH,
        )

    def dr_copy(s):
        to = ia_peer(s)
        return pltpu.make_async_remote_copy(
            src_ref=right_all.at[pl.ds(to * k_r, k_r)],
            dst_ref=dr_recv.at[s],
            send_sem=drsend.at[s],
            recv_sem=drrecv.at[s],
            device_id=(to, my_ja),
            device_id_type=MESH,
        )

    def each(copy, n, act):
        def body(s, c):
            act(copy(s))
            return c

        lax.fori_loop(1, n, body, 0)

    project(cols_piece, rows_j, k_r, wr_ref, save_r, right_all, my_ia * k_r)
    pl.semaphore_wait(barrier, n_ia + n_ja - 2)
    each(right_copy, n_ia, lambda c: c.start())
    for copy in ins[4:6]:
        copy.wait()

    def widen(r, c):
        xs_l[pl.ds(pl.multiple_of(r * pitch, 8), k_l), :] = slab_ref[r].astype(F32)
        return c

    lax.fori_loop(0, rows_i, widen, 0, unroll=4)
    project(slab_piece, rows_i, k_l, wl_ref, save_l, left_all, my_ja * k_l)
    each(left_copy, n_ja, lambda c: c.start())

    for copy in ins[6:]:
        copy.wait()
    ugain = ugain_ref[...]
    ubias = ubias_ref[...]
    t_rows = chunk_of(rows_i, rows_j, 128)
    t_flat = t_rows * rows_j

    def tile_slot(t):
        return pl.ds(pl.multiple_of(t * t_flat, 8), t_flat)

    def gate_body(t, c):
        x = tile_ref[pl.ds(t * t_rows, t_rows)].astype(F32).reshape(t_flat, ch)
        scaled, inverse = normalize(x)
        gate = jax.nn.sigmoid(dot((scaled * gain + bias).astype(BF16), wg_ref[...]))
        at = tile_slot(t)
        save_t[0, at, :] = scaled
        save_t[1, at, :] = jnp.broadcast_to(inverse, scaled.shape)
        save_t[2, at, :] = gate
        return c

    lax.fori_loop(0, rows_i // t_rows, gate_body, 0)

    each(right_copy, n_ia, lambda c: c.wait())

    block = math.gcd(rows_j, 8)

    def tri_chunk(s, c):
        @pl.when(s > 0)
        def _():
            left_copy(s).wait()

        k_first = lax.rem(my_ja - s + n_ja, n_ja) * k_l

        def to_f32(k, c):
            left_f[k] = left_all[k].astype(F32)
            right_f[k] = right_all[k].astype(F32)
            return c

        lax.fori_loop(k_first, k_first + k_l, to_f32, 0)
        for first in range(0, rows_j, block):

            def tri_body(k, accs, first=first):
                l = left_f[k_first + k]
                return tuple(
                    acc + right_f[k_first + k, pl.ds(first + j, 1), :] * l
                    for j, acc in enumerate(accs)
                )

            accs = tuple(tri_t[pl.ds((first + j) * rows_i, rows_i), :] for j in range(block))
            accs = lax.fori_loop(0, k_l, tri_body, accs, unroll=2)
            for j, acc in enumerate(accs):
                tri_t[pl.ds((first + j) * rows_i, rows_i), :] = acc
        return c

    tri_t[...] = jnp.zeros_like(tri_t)
    lax.fori_loop(0, n_ja, tri_chunk, 0)

    def tile_body(t, c):
        at = tile_slot(t)
        tri = jnp.concatenate(
            [tri_t[pl.ds(t * t_rows + u, rows_j, stride=rows_i), :] for u in range(t_rows)], axis=0
        )
        scaled, inverse = normalize(tri)
        outer = dot((scaled * ugain + ubias).astype(BF16), wo_ref[...])
        gate = save_t[2, at, :]
        update_ref[pl.ds(t * t_rows, t_rows)] = (
            (gate * outer).astype(BF16).reshape(t_rows, rows_j, ch)
        )
        cot = cot_ref[pl.ds(t * t_rows, t_rows)].astype(F32).reshape(t_flat, ch)
        d_outer = (cot * gate).astype(BF16)
        save_t[3, at, :] = cot * outer * gate * (1.0 - gate)
        d_tri = norm_back(scaled, inverse, dot_t(d_outer, wo_ref[...]), ugain)
        d_tri = d_tri.astype(BF16).astype(F32)
        dtri[at, :] = d_tri
        for u in range(t_rows):
            tri_t[pl.ds(t * t_rows + u, rows_j, stride=rows_i), :] = d_tri[
                u * rows_j : (u + 1) * rows_j
            ]
        return c

    lax.fori_loop(0, rows_i // t_rows, tile_body, 0)
    outs[0].start()

    def left_part(s):
        k_first = ja_peer(s) * k_l
        u_l = math.gcd(k_l, 4)

        def body(t, c):
            k0 = k_first + t * u_l
            accs = [None] * u_l
            for j in range(rows_j):
                d = tri_t[pl.ds(j * rows_i, rows_i), :]
                for u in range(u_l):
                    term = right_f[k0 + u, pl.ds(j, 1), :] * d
                    accs[u] = term if j == 0 else accs[u] + term
            for u in range(u_l):
                left_all[k0 + u] = accs[u].astype(BF16)
            return c

        lax.fori_loop(0, k_l // u_l, body, 0)

    def right_part(s):
        k_first = ia_peer(s) * k_r
        u_r = math.gcd(k_r, 4)

        def body(t, c):
            k0 = k_first + t * u_r
            accs = [None] * u_r
            for i in range(rows_i):
                d = dtri[pl.ds(i * rows_j, rows_j), :]
                for u in range(u_r):
                    term = left_f[k0 + u, pl.ds(i, 1), :] * d
                    accs[u] = term if i == 0 else accs[u] + term
            for u in range(u_r):
                right_all[k0 + u] = accs[u].astype(BF16)
            return c

        lax.fori_loop(0, k_r // u_r, body, 0)

    groups = min(n_ia, n_ja)

    def group_body(g, c):
        def one_right(v, c):
            s = g * (n_ia // groups) + v + 1
            right_part(s)

            @pl.when(s < n_ia)
            def _():
                dr_copy(s).start()

            return c

        def one_left(v, c):
            s = g * (n_ja // groups) + v + 1
            left_part(s)

            @pl.when(s < n_ja)
            def _():
                dl_copy(s).start()

            return c

        lax.fori_loop(0, n_ia // groups, one_right, 0)
        lax.fori_loop(0, n_ja // groups, one_left, 0)
        return c

    lax.fori_loop(0, groups, group_body, 0)

    def tile_back(t, c):
        at = tile_slot(t)
        grad = dot_t(save_t[3, at, :].astype(BF16), wg_ref[...])
        out = norm_back(save_t[0, at, :], save_t[1, at, :], grad, gain)
        gtile_ref[pl.ds(t * t_rows, t_rows)] = out.astype(BF16).reshape(t_rows, rows_j, ch)
        return c

    lax.fori_loop(0, rows_i // t_rows, tile_back, 0)
    outs[1].start()

    def project_back(put, rows, count, w_ref, save, edges, base, recv, n):
        step = chunk_of(count, rows, 256)

        def body(t, c):
            k0 = t * step
            at = pl.ds(pl.multiple_of(k0 * rows, 8), step * rows)
            d = edges[pl.ds(base + k0, step)].astype(F32)

            def add(s, d):
                return d + recv[s, pl.ds(k0, step)].astype(F32)

            d = lax.fori_loop(1, n, add, d, unroll=n <= 8).reshape(step * rows, ch)
            linear, sigma = save[2, at, :], save[3, at, :]
            p = jnp.concatenate([d * sigma, d * linear * sigma * (1.0 - sigma)], axis=-1)
            grad = dot_t(p.astype(BF16), w_ref[...])
            put(k0, step, norm_back(save[0, at, :], save[1, at, :], grad, gain))
            return c

        lax.fori_loop(0, count // step, body, 0)

    def put_cols(k0, step, out):
        gcols_ref[pl.ds(k0, step)] = out.astype(BF16).reshape(step, rows_j, ch)

    def put_slab(k0, step, out):
        for u in range(step):
            xs_l[pl.ds(k0 + u, rows_i, stride=pitch), :] = out[u * rows_i : (u + 1) * rows_i]

    each(dr_copy, n_ia, lambda c: c.wait())
    project_back(put_cols, rows_j, k_r, wr_ref, save_r, right_all, my_ia * k_r, dr_recv, n_ia)
    outs[2].start()
    each(dl_copy, n_ja, lambda c: c.wait())
    project_back(put_slab, rows_i, k_l, wl_ref, save_l, left_all, my_ja * k_l, dl_recv, n_ja)

    def narrow(r, c):
        gslab_ref[r] = xs_l[pl.ds(pl.multiple_of(r * pitch, 8), k_l), :].astype(BF16)
        return c

    lax.fori_loop(0, rows_i, narrow, 0, unroll=4)
    outs[3].start()
    for copy in outs:
        copy.wait()


def move(*refs):
    n = len(refs) // 2
    sem = refs[-1]
    copies = [pltpu.make_async_copy(refs[m], refs[n + m], sem.at[m]) for m in range(n)]
    for copy in copies:
        copy.start()
    for copy in copies:
        copy.wait()


def solution(mesh):
    n_ia, n_ja = mesh.shape["ia"], mesh.shape["ja"]

    def shards(slab, cols, tile, cot, wl, wr, wg, wo, gain, bias, ugain, ubias):
        cols = jnp.transpose(cols, (1, 0, 2))
        rows_i, k_l, ch = slab.shape
        k_r, rows_j, _ = cols.shape
        res = k_l * n_ja
        pitch = -(-k_l // 8) * 8
        anywhere = pl.BlockSpec(memory_space=pl.ANY)
        flat = rows_i * rows_j
        dma = pltpu.SemaphoreType.DMA
        ins = (
            slab, cols, tile, cot, wl, wr, wg, wo,
            gain[None, :], bias[None, :], ugain[None, :], ubias[None, :],
        )
        results = [jax.ShapeDtypeStruct(a.shape, BF16) for a in (tile, slab, cols, tile)]
        buffers = (
            [(a.shape, a.dtype) for a in ins]
            + [(a.shape, a.dtype) for a in results]
            + [
                ((rows_i * pitch, ch), F32),
                ((4, rows_i * k_l, ch), F32),
                ((4, rows_j * k_r, ch), F32),
                ((res, rows_i, ch), BF16),
                ((res, rows_j, ch), BF16),
                ((res, rows_i, ch), F32),
                ((res, rows_j, ch), F32),
                ((n_ja, k_l, rows_i, ch), BF16),
                ((n_ia, k_r, rows_j, ch), BF16),
                ((flat, ch), F32),
                ((flat, ch), F32),
                ((4, flat, ch), F32),
            ]
        )
        held = sum(math.prod(shape) * jnp.dtype(kind).itemsize for shape, kind in buffers)
        scratch = [pltpu.VMEM(shape, kind) for shape, kind in buffers]
        n_io = len(ins) + len(results)
        done = pl.pallas_call(
            functools.partial(kernel, n_ia, n_ja),
            out_shape=results,
            in_specs=[pl.BlockSpec(memory_space=pltpu.HBM)] * len(ins),
            out_specs=[anywhere] * len(results),
            scratch_shapes=scratch[:n_io]
            + [dma((len(ins),)), dma((len(results),))]
            + scratch[n_io:]
            + [dma((n,)) for n in (n_ja, n_ja, n_ia, n_ia, n_ja, n_ja, n_ia, n_ia)],
            compiler_params=pltpu.CompilerParams(
                collective_id=0, has_side_effects=True, vmem_limit_bytes=held + 4 * 1024 * 1024
            ),
        )(*ins)
        update, gslab, gcols, gtile = pl.pallas_call(
            move,
            out_shape=results,
            in_specs=[anywhere] * len(results),
            out_specs=[anywhere] * len(results),
            scratch_shapes=[dma((len(results),))],
        )(*done)
        return update, gslab, jnp.transpose(gcols, (1, 0, 2)), gtile

    return jax.shard_map(
        shards,
        mesh=mesh,
        in_specs=(
            P("ia", "ja", None),
            P("ja", "ia", None),
            P("ia", "ja", None),
            P("ia", "ja", None),
        )
        + (P(),) * 8,
        out_specs=(
            P("ia", "ja", None),
            P("ia", "ja", None),
            P("ja", "ia", None),
            P("ia", "ja", None),
        ),
        check_vma=False,
    )
```

```python
import functools
import math

import jax
import jax.numpy as jnp
from jax import lax
from jax.experimental import pallas as pl
from jax.experimental.pallas import tpu as pltpu
from jax.sharding import PartitionSpec as P

EPSILON = 1e-05
VMEM_BYTES = 56 * 1024 * 1024
MESH = pl.DeviceIdType.MESH
F32 = jnp.float32
BF16 = jnp.bfloat16


def chunk_of(count, rows, most):
    return max(d for d in range(1, count + 1) if count % d == 0 and (d * rows <= most or d == 1))


def normalize(values):
    centre = jnp.mean(values, axis=-1, keepdims=True)
    shifted = values - centre
    inverse = lax.rsqrt(jnp.mean(shifted * shifted, axis=-1, keepdims=True) + EPSILON)
    return shifted * inverse, inverse


def norm_back(scaled, inverse, grad_out, gain):
    grad_hat = grad_out * gain
    first_mean = jnp.mean(grad_hat, axis=-1, keepdims=True)
    second_mean = jnp.mean(grad_hat * scaled, axis=-1, keepdims=True)
    return inverse * (grad_hat - first_mean - scaled * second_mean)


def dot(a, b):
    return jnp.dot(a, b, preferred_element_type=F32)


def dot_t(a, b):
    return lax.dot_general(a, b, (((1,), (1,)), ((), ())), preferred_element_type=F32)


def kernel(
    n_ia,
    n_ja,
    slab_hbm,
    cols_hbm,
    tile_hbm,
    cot_hbm,
    wl_hbm,
    wr_hbm,
    wg_hbm,
    wo_hbm,
    gain_hbm,
    bias_hbm,
    ugain_hbm,
    ubias_hbm,
    update_hbm,
    gslab_hbm,
    gcols_hbm,
    gtile_hbm,
    slab_ref,
    cols_ref,
    tile_ref,
    cot_ref,
    wl_ref,
    wr_ref,
    wg_ref,
    wo_ref,
    gain_ref,
    bias_ref,
    ugain_ref,
    ubias_ref,
    update_ref,
    gslab_ref,
    gcols_ref,
    gtile_ref,
    in_sem,
    out_sem,
    xs_l,
    save_l,
    save_r,
    left_all,
    right_all,
    left_f,
    right_f,
    dl_recv,
    dr_recv,
    tri_t,
    dtri,
    save_t,
    lsend,
    lrecv,
    rsend,
    rrecv,
    dlsend,
    dlrecv,
    drsend,
    drrecv,
):
    my_ia, my_ja = lax.axis_index("ia"), lax.axis_index("ja")
    rows_i, k_l, ch = slab_ref.shape
    k_r, rows_j, _ = cols_ref.shape

    ins = [
        pltpu.make_async_copy(a, b, in_sem.at[n])
        for n, (a, b) in enumerate(
            [
                (cols_hbm, cols_ref),
                (wr_hbm, wr_ref),
                (gain_hbm, gain_ref),
                (bias_hbm, bias_ref),
                (slab_hbm, slab_ref),
                (wl_hbm, wl_ref),
                (tile_hbm, tile_ref),
                (wg_hbm, wg_ref),
                (cot_hbm, cot_ref),
                (wo_hbm, wo_ref),
                (ugain_hbm, ugain_ref),
                (ubias_hbm, ubias_ref),
            ]
        )
    ]
    outs = [
        pltpu.make_async_copy(a, b, out_sem.at[n])
        for n, (a, b) in enumerate(
            [
                (update_ref, update_hbm),
                (gtile_ref, gtile_hbm),
                (gcols_ref, gcols_hbm),
                (gslab_ref, gslab_hbm),
            ]
        )
    ]
    for copy in ins:
        copy.start()

    def ja_peer(s):
        return lax.rem(my_ja + s, n_ja)

    def ia_peer(s):
        return lax.rem(my_ia + s, n_ia)

    barrier = pltpu.get_barrier_semaphore()

    def greet_ja(s, c):
        pl.semaphore_signal(barrier, inc=1, device_id=(my_ia, ja_peer(s)), device_id_type=MESH)
        return c

    def greet_ia(s, c):
        pl.semaphore_signal(barrier, inc=1, device_id=(ia_peer(s), my_ja), device_id_type=MESH)
        return c

    lax.fori_loop(1, n_ja, greet_ja, 0)
    lax.fori_loop(1, n_ia, greet_ia, 0)

    for copy in ins[:4]:
        copy.wait()
    gain = gain_ref[...]
    bias = bias_ref[...]
    pitch = xs_l.shape[0] // rows_i

    def slab_piece(k0, step):
        return jnp.concatenate(
            [xs_l[pl.ds(k0 + u, rows_i, stride=pitch), :] for u in range(step)], axis=0
        )

    def cols_piece(k0, step):
        return cols_ref[pl.ds(k0, step)].astype(F32).reshape(step * rows_j, ch)

    def project(piece, rows, count, w_ref, save, edges, base):
        step = chunk_of(count, rows, 256)

        def body(t, c):
            k0 = t * step
            x = piece(k0, step)
            scaled, inverse = normalize(x)
            q = dot((scaled * gain + bias).astype(BF16), w_ref[...])
            linear = q[:, :ch]
            sigma = jax.nn.sigmoid(q[:, ch:])
            at = pl.ds(pl.multiple_of(k0 * rows, 8), step * rows)
            save[0, at, :] = scaled
            save[1, at, :] = jnp.broadcast_to(inverse, scaled.shape)
            save[2, at, :] = linear
            save[3, at, :] = sigma
            edge = (sigma * linear).astype(BF16)
            edges[pl.ds(base + k0, step)] = edge.reshape(step, rows, ch)
            return c

        lax.fori_loop(0, count // step, body, 0)

    def left_copy(s):
        own = left_all.at[pl.ds(my_ja * k_l, k_l)]
        return pltpu.make_async_remote_copy(
            src_ref=own,
            dst_ref=own,
            send_sem=lsend.at[s],
            recv_sem=lrecv.at[s],
            device_id=(my_ia, ja_peer(s)),
            device_id_type=MESH,
        )

    def right_copy(s):
        own = right_all.at[pl.ds(my_ia * k_r, k_r)]
        return pltpu.make_async_remote_copy(
            src_ref=own,
            dst_ref=own,
            send_sem=rsend.at[s],
            recv_sem=rrecv.at[s],
            device_id=(ia_peer(s), my_ja),
            device_id_type=MESH,
        )

    def dl_copy(s):
        to = ja_peer(s)
        return pltpu.make_async_remote_copy(
            src_ref=left_all.at[pl.ds(to * k_l, k_l)],
            dst_ref=dl_recv.at[s],
            send_sem=dlsend.at[s],
            recv_sem=dlrecv.at[s],
            device_id=(my_ia, to),
            device_id_type=MESH,
        )

    def dr_copy(s):
        to = ia_peer(s)
        return pltpu.make_async_remote_copy(
            src_ref=right_all.at[pl.ds(to * k_r, k_r)],
            dst_ref=dr_recv.at[s],
            send_sem=drsend.at[s],
            recv_sem=drrecv.at[s],
            device_id=(to, my_ja),
            device_id_type=MESH,
        )

    def each(copy, n, act):
        def body(s, c):
            act(copy(s))
            return c

        lax.fori_loop(1, n, body, 0)

    project(cols_piece, rows_j, k_r, wr_ref, save_r, right_all, my_ia * k_r)
    pl.semaphore_wait(barrier, n_ia + n_ja - 2)
    each(right_copy, n_ia, lambda c: c.start())
    for copy in ins[4:6]:
        copy.wait()

    def widen(r, c):
        xs_l[pl.ds(pl.multiple_of(r * pitch, 8), k_l), :] = slab_ref[r].astype(F32)
        return c

    lax.fori_loop(0, rows_i, widen, 0, unroll=4)
    project(slab_piece, rows_i, k_l, wl_ref, save_l, left_all, my_ja * k_l)
    each(left_copy, n_ja, lambda c: c.start())

    for copy in ins[6:]:
        copy.wait()
    ugain = ugain_ref[...]
    ubias = ubias_ref[...]
    t_rows = chunk_of(rows_i, rows_j, 128)
    t_flat = t_rows * rows_j

    def tile_slot(t):
        return pl.ds(pl.multiple_of(t * t_flat, 8), t_flat)

    def gate_body(t, c):
        x = tile_ref[pl.ds(t * t_rows, t_rows)].astype(F32).reshape(t_flat, ch)
        scaled, inverse = normalize(x)
        gate = jax.nn.sigmoid(dot((scaled * gain + bias).astype(BF16), wg_ref[...]))
        at = tile_slot(t)
        save_t[0, at, :] = scaled
        save_t[1, at, :] = jnp.broadcast_to(inverse, scaled.shape)
        save_t[2, at, :] = gate
        return c

    lax.fori_loop(0, rows_i // t_rows, gate_body, 0)

    each(right_copy, n_ia, lambda c: c.wait())

    block = math.gcd(rows_j, 8)

    def tri_chunk(s, c):
        @pl.when(s > 0)
        def _():
            left_copy(s).wait()

        k_first = lax.rem(my_ja - s + n_ja, n_ja) * k_l

        def to_f32(k, c):
            left_f[k] = left_all[k].astype(F32)
            right_f[k] = right_all[k].astype(F32)
            return c

        lax.fori_loop(k_first, k_first + k_l, to_f32, 0)
        for first in range(0, rows_j, block):

            def tri_body(k, accs, first=first):
                l = left_f[k_first + k]
                return tuple(
                    acc + right_f[k_first + k, pl.ds(first + j, 1), :] * l
                    for j, acc in enumerate(accs)
                )

            accs = tuple(tri_t[pl.ds((first + j) * rows_i, rows_i), :] for j in range(block))
            accs = lax.fori_loop(0, k_l, tri_body, accs, unroll=2)
            for j, acc in enumerate(accs):
                tri_t[pl.ds((first + j) * rows_i, rows_i), :] = acc
        return c

    tri_t[...] = jnp.zeros_like(tri_t)
    lax.fori_loop(0, n_ja, tri_chunk, 0)

    def tile_body(t, c):
        at = tile_slot(t)
        tri = jnp.concatenate(
            [tri_t[pl.ds(t * t_rows + u, rows_j, stride=rows_i), :] for u in range(t_rows)], axis=0
        )
        scaled, inverse = normalize(tri)
        outer = dot((scaled * ugain + ubias).astype(BF16), wo_ref[...])
        gate = save_t[2, at, :]
        update_ref[pl.ds(t * t_rows, t_rows)] = (
            (gate * outer).astype(BF16).reshape(t_rows, rows_j, ch)
        )
        cot = cot_ref[pl.ds(t * t_rows, t_rows)].astype(F32).reshape(t_flat, ch)
        d_outer = (cot * gate).astype(BF16)
        save_t[3, at, :] = cot * outer * gate * (1.0 - gate)
        d_tri = norm_back(scaled, inverse, dot_t(d_outer, wo_ref[...]), ugain)
        d_tri = d_tri.astype(BF16).astype(F32)
        dtri[at, :] = d_tri
        for u in range(t_rows):
            tri_t[pl.ds(t * t_rows + u, rows_j, stride=rows_i), :] = d_tri[
                u * rows_j : (u + 1) * rows_j
            ]
        return c

    lax.fori_loop(0, rows_i // t_rows, tile_body, 0)
    outs[0].start()

    def left_part(s):
        k_first = ja_peer(s) * k_l
        u_l = math.gcd(k_l, 4)

        def body(t, c):
            k0 = k_first + t * u_l
            accs = [None] * u_l
            for j in range(rows_j):
                d = tri_t[pl.ds(j * rows_i, rows_i), :]
                for u in range(u_l):
                    term = right_f[k0 + u, pl.ds(j, 1), :] * d
                    accs[u] = term if j == 0 else accs[u] + term
            for u in range(u_l):
                left_all[k0 + u] = accs[u].astype(BF16)
            return c

        lax.fori_loop(0, k_l // u_l, body, 0)

    def right_part(s):
        k_first = ia_peer(s) * k_r
        u_r = math.gcd(k_r, 4)

        def body(t, c):
            k0 = k_first + t * u_r
            accs = [None] * u_r
            for i in range(rows_i):
                d = dtri[pl.ds(i * rows_j, rows_j), :]
                for u in range(u_r):
                    term = left_f[k0 + u, pl.ds(i, 1), :] * d
                    accs[u] = term if i == 0 else accs[u] + term
            for u in range(u_r):
                right_all[k0 + u] = accs[u].astype(BF16)
            return c

        lax.fori_loop(0, k_r // u_r, body, 0)

    groups = min(n_ia, n_ja)

    def group_body(g, c):
        def one_right(v, c):
            s = g * (n_ia // groups) + v + 1
            right_part(s)

            @pl.when(s < n_ia)
            def _():
                dr_copy(s).start()

            return c

        def one_left(v, c):
            s = g * (n_ja // groups) + v + 1
            left_part(s)

            @pl.when(s < n_ja)
            def _():
                dl_copy(s).start()

            return c

        lax.fori_loop(0, n_ia // groups, one_right, 0)
        lax.fori_loop(0, n_ja // groups, one_left, 0)
        return c

    lax.fori_loop(0, groups, group_body, 0)

    def tile_back(t, c):
        at = tile_slot(t)
        grad = dot_t(save_t[3, at, :].astype(BF16), wg_ref[...])
        out = norm_back(save_t[0, at, :], save_t[1, at, :], grad, gain)
        gtile_ref[pl.ds(t * t_rows, t_rows)] = out.astype(BF16).reshape(t_rows, rows_j, ch)
        return c

    lax.fori_loop(0, rows_i // t_rows, tile_back, 0)
    outs[1].start()

    def project_back(put, rows, count, w_ref, save, edges, base, recv, n):
        step = chunk_of(count, rows, 256)

        def body(t, c):
            k0 = t * step
            at = pl.ds(pl.multiple_of(k0 * rows, 8), step * rows)
            d = edges[pl.ds(base + k0, step)].astype(F32)

            def add(s, d):
                return d + recv[s, pl.ds(k0, step)].astype(F32)

            d = lax.fori_loop(1, n, add, d, unroll=n <= 8).reshape(step * rows, ch)
            linear, sigma = save[2, at, :], save[3, at, :]
            p = jnp.concatenate([d * sigma, d * linear * sigma * (1.0 - sigma)], axis=-1)
            grad = dot_t(p.astype(BF16), w_ref[...])
            put(k0, step, norm_back(save[0, at, :], save[1, at, :], grad, gain))
            return c

        lax.fori_loop(0, count // step, body, 0)

    def put_cols(k0, step, out):
        gcols_ref[pl.ds(k0, step)] = out.astype(BF16).reshape(step, rows_j, ch)

    def put_slab(k0, step, out):
        for u in range(step):
            xs_l[pl.ds(k0 + u, rows_i, stride=pitch), :] = out[u * rows_i : (u + 1) * rows_i]

    each(dr_copy, n_ia, lambda c: c.wait())
    project_back(put_cols, rows_j, k_r, wr_ref, save_r, right_all, my_ia * k_r, dr_recv, n_ia)
    outs[2].start()
    each(dl_copy, n_ja, lambda c: c.wait())
    project_back(put_slab, rows_i, k_l, wl_ref, save_l, left_all, my_ja * k_l, dl_recv, n_ja)

    def narrow(r, c):
        gslab_ref[r] = xs_l[pl.ds(pl.multiple_of(r * pitch, 8), k_l), :].astype(BF16)
        return c

    lax.fori_loop(0, rows_i, narrow, 0, unroll=4)
    outs[3].start()
    for copy in outs:
        copy.wait()


def move(*refs):
    n = (len(refs) - 2) // 3
    came, left = refs[-2], refs[-1]
    takes = [pltpu.make_async_copy(refs[m], refs[2 * n + m], came.at[m]) for m in range(n)]
    gives = [pltpu.make_async_copy(refs[2 * n + m], refs[n + m], left.at[m]) for m in range(n)]
    for copy in takes:
        copy.start()
    for take, give in zip(takes, gives):
        take.wait()
        give.start()
    for copy in gives:
        copy.wait()


def solution(mesh):
    n_ia, n_ja = mesh.shape["ia"], mesh.shape["ja"]

    def shards(slab, cols, tile, cot, wl, wr, wg, wo, gain, bias, ugain, ubias):
        cols = jnp.transpose(cols, (1, 0, 2))
        rows_i, k_l, ch = slab.shape
        k_r, rows_j, _ = cols.shape
        res = k_l * n_ja
        pitch = -(-k_l // 8) * 8
        anywhere = pl.BlockSpec(memory_space=pl.ANY)
        flat = rows_i * rows_j
        dma = pltpu.SemaphoreType.DMA
        ins = (
            slab, cols, tile, cot, wl, wr, wg, wo,
            gain[None, :], bias[None, :], ugain[None, :], ubias[None, :],
        )
        results = [jax.ShapeDtypeStruct(a.shape, BF16) for a in (tile, slab, cols, tile)]
        buffers = (
            [(a.shape, a.dtype) for a in ins]
            + [(a.shape, a.dtype) for a in results]
            + [
                ((rows_i * pitch, ch), F32),
                ((4, rows_i * k_l, ch), F32),
                ((4, rows_j * k_r, ch), F32),
                ((res, rows_i, ch), BF16),
                ((res, rows_j, ch), BF16),
                ((res, rows_i, ch), F32),
                ((res, rows_j, ch), F32),
                ((n_ja, k_l, rows_i, ch), BF16),
                ((n_ia, k_r, rows_j, ch), BF16),
                ((flat, ch), F32),
                ((flat, ch), F32),
                ((4, flat, ch), F32),
            ]
        )
        scratch = [pltpu.VMEM(shape, kind) for shape, kind in buffers]
        n_io = len(ins) + len(results)
        done = pl.pallas_call(
            functools.partial(kernel, n_ia, n_ja),
            out_shape=results,
            in_specs=[pl.BlockSpec(memory_space=pltpu.HBM)] * len(ins),
            out_specs=[anywhere] * len(results),
            scratch_shapes=scratch[:n_io]
            + [dma((len(ins),)), dma((len(results),))]
            + scratch[n_io:]
            + [dma((n,)) for n in (n_ja, n_ja, n_ia, n_ia, n_ja, n_ja, n_ia, n_ia)],
            compiler_params=pltpu.CompilerParams(
                collective_id=0, has_side_effects=True, vmem_limit_bytes=VMEM_BYTES
            ),
        )(*ins)
        update, gslab, gcols, gtile = pl.pallas_call(
            move,
            out_shape=results,
            in_specs=[anywhere] * len(results),
            out_specs=[anywhere] * len(results),
            scratch_shapes=scratch[len(ins) : n_io] + [dma((len(results),))] * 2,
            compiler_params=pltpu.CompilerParams(vmem_limit_bytes=VMEM_BYTES),
        )(*done)
        return update, gslab, jnp.transpose(gcols, (1, 0, 2)), gtile

    return jax.shard_map(
        shards,
        mesh=mesh,
        in_specs=(
            P("ia", "ja", None),
            P("ja", "ia", None),
            P("ia", "ja", None),
            P("ia", "ja", None),
        )
        + (P(),) * 8,
        out_specs=(
            P("ia", "ja", None),
            P("ia", "ja", None),
            P("ja", "ia", None),
            P("ia", "ja", None),
        ),
        check_vma=False,
    )
```

```python
import functools
import math

import jax
import jax.numpy as jnp
from jax import lax
from jax.experimental import pallas as pl
from jax.experimental.pallas import tpu as pltpu
from jax.sharding import PartitionSpec as P

EPSILON = 1e-05
VMEM_BYTES = 56 * 1024 * 1024
MESH = pl.DeviceIdType.MESH
F32 = jnp.float32
BF16 = jnp.bfloat16


def chunk_of(count, rows, most):
    return max(d for d in range(1, count + 1) if count % d == 0 and (d * rows <= most or d == 1))


def normalize(values):
    centre = jnp.mean(values, axis=-1, keepdims=True)
    shifted = values - centre
    inverse = lax.rsqrt(jnp.mean(shifted * shifted, axis=-1, keepdims=True) + EPSILON)
    return shifted * inverse, inverse


def norm_back(scaled, inverse, grad_out, gain):
    grad_hat = grad_out * gain
    first_mean = jnp.mean(grad_hat, axis=-1, keepdims=True)
    second_mean = jnp.mean(grad_hat * scaled, axis=-1, keepdims=True)
    return inverse * (grad_hat - first_mean - scaled * second_mean)


def dot(a, b):
    return jnp.dot(a, b, preferred_element_type=F32)


def dot_t(a, b):
    return lax.dot_general(a, b, (((1,), (1,)), ((), ())), preferred_element_type=F32)


def kernel(
    n_ia,
    n_ja,
    slab_hbm,
    cols_hbm,
    tile_hbm,
    cot_hbm,
    wl_hbm,
    wr_hbm,
    wg_hbm,
    wo_hbm,
    gain_hbm,
    bias_hbm,
    ugain_hbm,
    ubias_hbm,
    update_hbm,
    gslab_hbm,
    gcols_hbm,
    gtile_hbm,
    slab_ref,
    cols_ref,
    tile_ref,
    cot_ref,
    wl_ref,
    wr_ref,
    wg_ref,
    wo_ref,
    gain_ref,
    bias_ref,
    ugain_ref,
    ubias_ref,
    update_ref,
    gslab_ref,
    gcols_ref,
    gtile_ref,
    in_sem,
    out_sem,
    xs_l,
    save_l,
    save_r,
    left_all,
    right_all,
    left_f,
    right_f,
    dl_recv,
    dr_recv,
    tri_t,
    dtri,
    save_t,
    lsend,
    lrecv,
    rsend,
    rrecv,
    fsend,
    frecv,
    dlsend,
    dlrecv,
    drsend,
    drrecv,
    sibsend,
    sibrecv,
):
    my_ia, my_ja = lax.axis_index("ia"), lax.axis_index("ja")
    rows_i, k_l, ch = slab_ref.shape
    k_r, rows_j, _ = cols_ref.shape

    ins = [
        pltpu.make_async_copy(a, b, in_sem.at[n])
        for n, (a, b) in enumerate(
            [
                (cols_hbm, cols_ref),
                (wr_hbm, wr_ref),
                (gain_hbm, gain_ref),
                (bias_hbm, bias_ref),
                (slab_hbm, slab_ref),
                (wl_hbm, wl_ref),
                (tile_hbm, tile_ref),
                (wg_hbm, wg_ref),
                (cot_hbm, cot_ref),
                (wo_hbm, wo_ref),
                (ugain_hbm, ugain_ref),
                (ubias_hbm, ubias_ref),
            ]
        )
    ]
    outs = [
        pltpu.make_async_copy(a, b, out_sem.at[n])
        for n, (a, b) in enumerate(
            [
                (update_ref, update_hbm),
                (gtile_ref, gtile_hbm),
                (gcols_ref, gcols_hbm),
                (gslab_ref, gslab_hbm),
            ]
        )
    ]
    for copy in ins:
        copy.start()

    n_z = n_ia // 2
    my_z, my_core = my_ia // 2, lax.rem(my_ia, 2)
    sibling = my_z * 2 + 1 - my_core
    square = n_ja == 4 and k_l % 2 == 0
    half = k_l // 2

    def ja_peer(s):
        if square:
            return lax.rem(my_ja // 2 + s // 2, 2) * 2 + lax.rem(my_ja + s, 2)
        return lax.rem(my_ja + s, n_ja)

    def ia_peer(s):
        return lax.rem(my_ia + s, n_ia)

    def z_peer(s):
        return lax.rem(my_z + s, n_z)

    barrier = pltpu.get_barrier_semaphore()

    def greet_ja(s, c):
        pl.semaphore_signal(barrier, inc=1, device_id=(my_ia, ja_peer(s)), device_id_type=MESH)
        return c

    def greet_ia(s, c):
        pl.semaphore_signal(barrier, inc=1, device_id=(ia_peer(s), my_ja), device_id_type=MESH)
        return c

    lax.fori_loop(1, n_ja, greet_ja, 0)
    lax.fori_loop(1, n_ia, greet_ia, 0)

    for copy in ins[:4]:
        copy.wait()
    gain = gain_ref[...]
    bias = bias_ref[...]
    pitch = xs_l.shape[0] // rows_i

    def slab_piece(k0, step):
        return jnp.concatenate(
            [xs_l[pl.ds(k0 + u, rows_i, stride=pitch), :] for u in range(step)], axis=0
        )

    def cols_piece(k0, step):
        return cols_ref[pl.ds(k0, step)].astype(F32).reshape(step * rows_j, ch)

    def project(piece, rows, count, w_ref, save, edges, base):
        step = chunk_of(count, rows, 256)

        def body(t, c):
            k0 = t * step
            x = piece(k0, step)
            scaled, inverse = normalize(x)
            q = dot((scaled * gain + bias).astype(BF16), w_ref[...])
            linear = q[:, :ch]
            sigma = jax.nn.sigmoid(q[:, ch:])
            at = pl.ds(pl.multiple_of(k0 * rows, 8), step * rows)
            save[0, at, :] = scaled
            save[1, at, :] = jnp.broadcast_to(inverse, scaled.shape)
            save[2, at, :] = linear
            save[3, at, :] = sigma
            edge = (sigma * linear).astype(BF16)
            edges[pl.ds(base + k0, step)] = edge.reshape(step, rows, ch)
            return c

        lax.fori_loop(0, count // step, body, 0)

    def left_copy(s):
        own = left_all.at[pl.ds(my_ja * k_l, k_l)]
        return pltpu.make_async_remote_copy(
            src_ref=own,
            dst_ref=own,
            send_sem=lsend.at[s],
            recv_sem=lrecv.at[s],
            device_id=(my_ia, ja_peer(s)),
            device_id_type=MESH,
        )

    def left_hop(m):
        owner, part, to = ((0, 0, 1), (0, 1, 2), (0, 1, 1), (0, 0, 2), (1, 0, 2), (2, 1, 1))[m]
        piece = left_all.at[pl.ds(ja_peer(owner) * k_l + part * half, half)]
        return pltpu.make_async_remote_copy(
            src_ref=piece,
            dst_ref=piece,
            send_sem=lsend.at[m],
            recv_sem=lrecv.at[m],
            device_id=(my_ia, ja_peer(to)),
            device_id_type=MESH,
        )

    def right_copy(s):
        own = right_all.at[pl.ds(my_ia * k_r, k_r)]
        return pltpu.make_async_remote_copy(
            src_ref=own,
            dst_ref=own,
            send_sem=rsend.at[s],
            recv_sem=rrecv.at[s],
            device_id=(z_peer(s) * 2 + my_core, my_ja),
            device_id_type=MESH,
        )

    def right_forward(s):
        piece = right_all.at[pl.ds((z_peer(n_z - s) * 2 + my_core) * k_r, k_r)]
        return pltpu.make_async_remote_copy(
            src_ref=piece,
            dst_ref=piece,
            send_sem=fsend.at[s],
            recv_sem=frecv.at[s],
            device_id=(sibling, my_ja),
            device_id_type=MESH,
        )

    def dl_copy(s):
        to = ja_peer(s)
        return pltpu.make_async_remote_copy(
            src_ref=left_all.at[pl.ds(to * k_l, k_l)],
            dst_ref=dl_recv.at[s],
            send_sem=dlsend.at[s],
            recv_sem=dlrecv.at[s],
            device_id=(my_ia, to),
            device_id_type=MESH,
        )

    def dl_hop(m):
        piece, part, to, slot = (
            (3, 0, 1, 3), (3, 1, 2, 3), (1, 0, 1, 1), (2, 1, 2, 2), (1, 1, 1, 1), (2, 0, 2, 2),
        )[m]
        return pltpu.make_async_remote_copy(
            src_ref=left_all.at[pl.ds(ja_peer(piece) * k_l + part * half, half)],
            dst_ref=dl_recv.at[slot, pl.ds(part * half, half)],
            send_sem=dlsend.at[m],
            recv_sem=dlrecv.at[m],
            device_id=(my_ia, ja_peer(to)),
            device_id_type=MESH,
        )

    def dr_sibling(s):
        return pltpu.make_async_remote_copy(
            src_ref=right_all.at[pl.ds((z_peer(s) * 2 + 1 - my_core) * k_r, k_r)],
            dst_ref=dr_recv.at[n_z + s],
            send_sem=sibsend.at[s],
            recv_sem=sibrecv.at[s],
            device_id=(sibling, my_ja),
            device_id_type=MESH,
        )

    def dr_copy(s):
        to = z_peer(s) * 2 + my_core
        return pltpu.make_async_remote_copy(
            src_ref=right_all.at[pl.ds(to * k_r, k_r)],
            dst_ref=dr_recv.at[s],
            send_sem=drsend.at[s],
            recv_sem=drrecv.at[s],
            device_id=(to, my_ja),
            device_id_type=MESH,
        )

    def each(copy, n, act):
        def body(s, c):
            act(copy(s))
            return c

        lax.fori_loop(1, n, body, 0)

    project(cols_piece, rows_j, k_r, wr_ref, save_r, right_all, my_ia * k_r)
    pl.semaphore_wait(barrier, n_ia + n_ja - 2)
    each(right_copy, n_z, lambda c: c.start())
    right_forward(0).start()
    for copy in ins[4:6]:
        copy.wait()

    def widen(r, c):
        xs_l[pl.ds(pl.multiple_of(r * pitch, 8), k_l), :] = slab_ref[r].astype(F32)
        return c

    lax.fori_loop(0, rows_i, widen, 0, unroll=4)
    project(slab_piece, rows_i, k_l, wl_ref, save_l, left_all, my_ja * k_l)
    if square:
        for m in range(4):
            left_hop(m).start()
    else:
        each(left_copy, n_ja, lambda c: c.start())

    for copy in ins[6:]:
        copy.wait()
    ugain = ugain_ref[...]
    ubias = ubias_ref[...]
    t_rows = chunk_of(rows_i, rows_j, 128)
    t_flat = t_rows * rows_j

    def tile_slot(t):
        return pl.ds(pl.multiple_of(t * t_flat, 8), t_flat)

    def gate_body(t, c):
        x = tile_ref[pl.ds(t * t_rows, t_rows)].astype(F32).reshape(t_flat, ch)
        scaled, inverse = normalize(x)
        gate = jax.nn.sigmoid(dot((scaled * gain + bias).astype(BF16), wg_ref[...]))
        at = tile_slot(t)
        save_t[0, at, :] = scaled
        save_t[1, at, :] = jnp.broadcast_to(inverse, scaled.shape)
        save_t[2, at, :] = gate
        return c

    lax.fori_loop(0, rows_i // t_rows, gate_body, 0)

    def pass_on(s, c):
        right_copy(s).wait_recv()
        right_forward(s).start()
        return c

    lax.fori_loop(1, n_z, pass_on, 0)
    if square:
        left_hop(0).wait_recv()
        left_hop(4).start()
        left_hop(1).wait_recv()
        left_hop(5).start()
    each(right_copy, n_z, lambda c: c.wait_send())
    lax.fori_loop(0, n_z, lambda s, c: (right_forward(s).wait(), c)[1], 0)

    block = math.gcd(rows_j, 8)

    def tri_chunk(s, c):
        if square:

            @pl.when(s == 1)
            def _():
                left_hop(2).wait_recv()

            @pl.when(s == 2)
            def _():
                left_hop(3).wait_recv()

            @pl.when(s == 3)
            def _():
                left_hop(4).wait_recv()
                left_hop(5).wait_recv()

            k_first = ja_peer(s) * k_l
        else:

            @pl.when(s > 0)
            def _():
                left_copy(s).wait()

            k_first = ja_peer(n_ja - s) * k_l

        def to_f32(k, c):
            left_f[k] = left_all[k].astype(F32)
            right_f[k] = right_all[k].astype(F32)
            return c

        lax.fori_loop(k_first, k_first + k_l, to_f32, 0)
        for first in range(0, rows_j, block):

            def tri_body(k, accs, first=first):
                l = left_f[k_first + k]
                return tuple(
                    acc + right_f[k_first + k, pl.ds(first + j, 1), :] * l
                    for j, acc in enumerate(accs)
                )

            accs = tuple(tri_t[pl.ds((first + j) * rows_i, rows_i), :] for j in range(block))
            accs = lax.fori_loop(0, k_l, tri_body, accs, unroll=2)
            for j, acc in enumerate(accs):
                tri_t[pl.ds((first + j) * rows_i, rows_i), :] = acc
        return c

    tri_t[...] = jnp.zeros_like(tri_t)
    lax.fori_loop(0, n_ja, tri_chunk, 0)
    if square:
        for m in range(6):
            left_hop(m).wait_send()

    def tile_body(t, c):
        at = tile_slot(t)
        tri = jnp.concatenate(
            [tri_t[pl.ds(t * t_rows + u, rows_j, stride=rows_i), :] for u in range(t_rows)], axis=0
        )
        scaled, inverse = normalize(tri)
        outer = dot((scaled * ugain + ubias).astype(BF16), wo_ref[...])
        gate = save_t[2, at, :]
        update_ref[pl.ds(t * t_rows, t_rows)] = (
            (gate * outer).astype(BF16).reshape(t_rows, rows_j, ch)
        )
        cot = cot_ref[pl.ds(t * t_rows, t_rows)].astype(F32).reshape(t_flat, ch)
        d_outer = (cot * gate).astype(BF16)
        save_t[3, at, :] = cot * outer * gate * (1.0 - gate)
        d_tri = norm_back(scaled, inverse, dot_t(d_outer, wo_ref[...]), ugain)
        d_tri = d_tri.astype(BF16).astype(F32)
        dtri[at, :] = d_tri
        for u in range(t_rows):
            tri_t[pl.ds(t * t_rows + u, rows_j, stride=rows_i), :] = d_tri[
                u * rows_j : (u + 1) * rows_j
            ]
        return c

    lax.fori_loop(0, rows_i // t_rows, tile_body, 0)
    outs[0].start()

    def left_part(s):
        k_first = ja_peer(s) * k_l
        u_l = math.gcd(k_l, 4)

        def body(t, c):
            k0 = k_first + t * u_l
            accs = [None] * u_l
            for j in range(rows_j):
                d = tri_t[pl.ds(j * rows_i, rows_i), :]
                for u in range(u_l):
                    term = right_f[k0 + u, pl.ds(j, 1), :] * d
                    accs[u] = term if j == 0 else accs[u] + term
            for u in range(u_l):
                left_all[k0 + u] = accs[u].astype(BF16)
            return c

        lax.fori_loop(0, k_l // u_l, body, 0)

    def right_part(to, came=None):
        k_first = to * k_r
        u_r = math.gcd(k_r, 4)

        def body(t, c):
            k0 = k_first + t * u_r
            accs = [None] * u_r
            for i in range(rows_i):
                d = dtri[pl.ds(i * rows_j, rows_j), :]
                for u in range(u_r):
                    term = left_f[k0 + u, pl.ds(i, 1), :] * d
                    accs[u] = term if i == 0 else accs[u] + term
            for u in range(u_r):
                acc = accs[u]
                if came is not None:
                    acc = acc + dr_recv[came, t * u_r + u].astype(F32)
                right_all[k0 + u] = acc.astype(BF16)
            return c

        lax.fori_loop(0, k_r // u_r, body, 0)

    def for_sibling(v, c):
        s = lax.rem(v + 1, n_z)
        right_part(z_peer(s) * 2 + 1 - my_core)
        dr_sibling(s).start()
        return c

    def for_core(s, c):
        dr_sibling(s).wait_recv()
        right_part(z_peer(s) * 2 + my_core, n_z + s)
        dr_copy(s).start()
        return c

    def for_ja(s, c):
        left_part(s)
        dl_copy(s).start()
        return c

    def add_half(slot, part):
        at = pl.ds(ja_peer(slot) * k_l + part * half, half)
        mine = left_all[at].astype(F32)
        came = dl_recv[3, pl.ds(part * half, half)].astype(F32)
        left_all[at] = (mine + came).astype(BF16)

    if square:
        left_part(3)
        dl_hop(0).start()
        dl_hop(1).start()
        lax.fori_loop(0, n_z, for_sibling, 0)
        left_part(1)
        dl_hop(2).start()
        left_part(2)
        dl_hop(3).start()
        lax.fori_loop(1, n_z, for_core, 0)
        dl_hop(0).wait_recv()
        add_half(2, 0)
        dl_hop(5).start()
        dl_hop(1).wait_recv()
        add_half(1, 1)
        dl_hop(4).start()
    else:
        lax.fori_loop(0, n_z, for_sibling, 0)
        lax.fori_loop(1, n_z, for_core, 0)
        lax.fori_loop(1, n_ja, for_ja, 0)
    left_part(0)
    dr_sibling(0).wait_recv()
    right_part(my_ia)

    def tile_back(t, c):
        at = tile_slot(t)
        grad = dot_t(save_t[3, at, :].astype(BF16), wg_ref[...])
        out = norm_back(save_t[0, at, :], save_t[1, at, :], grad, gain)
        gtile_ref[pl.ds(t * t_rows, t_rows)] = out.astype(BF16).reshape(t_rows, rows_j, ch)
        return c

    lax.fori_loop(0, rows_i // t_rows, tile_back, 0)
    outs[1].start()

    def project_back(put, rows, count, w_ref, save, edges, base, recv, first, n):
        step = chunk_of(count, rows, 256)

        def body(t, c):
            k0 = t * step
            at = pl.ds(pl.multiple_of(k0 * rows, 8), step * rows)
            d = edges[pl.ds(base + k0, step)].astype(F32)

            def add(s, d):
                return d + recv[s, pl.ds(k0, step)].astype(F32)

            d = lax.fori_loop(first, n, add, d, unroll=n <= 8).reshape(step * rows, ch)
            linear, sigma = save[2, at, :], save[3, at, :]
            p = jnp.concatenate([d * sigma, d * linear * sigma * (1.0 - sigma)], axis=-1)
            grad = dot_t(p.astype(BF16), w_ref[...])
            put(k0, step, norm_back(save[0, at, :], save[1, at, :], grad, gain))
            return c

        lax.fori_loop(0, count // step, body, 0)

    def put_cols(k0, step, out):
        gcols_ref[pl.ds(k0, step)] = out.astype(BF16).reshape(step, rows_j, ch)

    def put_slab(k0, step, out):
        for u in range(step):
            xs_l[pl.ds(k0 + u, rows_i, stride=pitch), :] = out[u * rows_i : (u + 1) * rows_i]

    each(dr_copy, n_z, lambda c: c.wait())
    lax.fori_loop(0, n_z, lambda s, c: (dr_sibling(s).wait_send(), c)[1], 0)
    project_back(put_cols, rows_j, k_r, wr_ref, save_r, right_all, my_ia * k_r, dr_recv, 1, n_z + 1)
    outs[2].start()
    if square:
        for m in range(6):
            dl_hop(m).wait_send()
        for m in range(2, 6):
            dl_hop(m).wait_recv()
    else:
        each(dl_copy, n_ja, lambda c: c.wait())
    last = 3 if square else n_ja
    project_back(put_slab, rows_i, k_l, wl_ref, save_l, left_all, my_ja * k_l, dl_recv, 1, last)

    def narrow(r, c):
        gslab_ref[r] = xs_l[pl.ds(pl.multiple_of(r * pitch, 8), k_l), :].astype(BF16)
        return c

    lax.fori_loop(0, rows_i, narrow, 0, unroll=4)
    outs[3].start()
    for copy in outs:
        copy.wait()


def move(*refs):
    n = (len(refs) - 2) // 3
    came, left = refs[-2], refs[-1]
    takes = [pltpu.make_async_copy(refs[m], refs[2 * n + m], came.at[m]) for m in range(n)]
    gives = [pltpu.make_async_copy(refs[2 * n + m], refs[n + m], left.at[m]) for m in range(n)]
    for copy in takes:
        copy.start()
    for take, give in zip(takes, gives):
        take.wait()
        give.start()
    for copy in gives:
        copy.wait()


def solution(mesh):
    n_ia, n_ja = mesh.shape["ia"], mesh.shape["ja"]

    def shards(slab, cols, tile, cot, wl, wr, wg, wo, gain, bias, ugain, ubias):
        cols = jnp.transpose(cols, (1, 0, 2))
        rows_i, k_l, ch = slab.shape
        k_r, rows_j, _ = cols.shape
        res = k_l * n_ja
        pitch = -(-k_l // 8) * 8
        anywhere = pl.BlockSpec(memory_space=pl.ANY)
        flat = rows_i * rows_j
        dma = pltpu.SemaphoreType.DMA
        ins = (
            slab, cols, tile, cot, wl, wr, wg, wo,
            gain[None, :], bias[None, :], ugain[None, :], ubias[None, :],
        )
        results = [jax.ShapeDtypeStruct(a.shape, BF16) for a in (tile, slab, cols, tile)]
        buffers = (
            [(a.shape, a.dtype) for a in ins]
            + [(a.shape, a.dtype) for a in results]
            + [
                ((rows_i * pitch, ch), F32),
                ((4, rows_i * k_l, ch), F32),
                ((4, rows_j * k_r, ch), F32),
                ((res, rows_i, ch), BF16),
                ((res, rows_j, ch), BF16),
                ((res, rows_i, ch), F32),
                ((res, rows_j, ch), F32),
                ((n_ja, k_l, rows_i, ch), BF16),
                ((n_ia, k_r, rows_j, ch), BF16),
                ((flat, ch), F32),
                ((flat, ch), F32),
                ((4, flat, ch), F32),
            ]
        )
        scratch = [pltpu.VMEM(shape, kind) for shape, kind in buffers]
        n_io = len(ins) + len(results)
        done = pl.pallas_call(
            functools.partial(kernel, n_ia, n_ja),
            out_shape=results,
            in_specs=[pl.BlockSpec(memory_space=pltpu.HBM)] * len(ins),
            out_specs=[anywhere] * len(results),
            scratch_shapes=scratch[:n_io]
            + [dma((len(ins),)), dma((len(results),))]
            + scratch[n_io:]
            + [dma((n,)) for n in (n_ja + 2, n_ja + 2, n_ia, n_ia, n_ia, n_ia) * 2],
            compiler_params=pltpu.CompilerParams(
                collective_id=0, has_side_effects=True, vmem_limit_bytes=VMEM_BYTES
            ),
        )(*ins)
        update, gslab, gcols, gtile = pl.pallas_call(
            move,
            out_shape=results,
            in_specs=[anywhere] * len(results),
            out_specs=[anywhere] * len(results),
            scratch_shapes=scratch[len(ins) : n_io] + [dma((len(results),))] * 2,
            compiler_params=pltpu.CompilerParams(vmem_limit_bytes=VMEM_BYTES),
        )(*done)
        return update, gslab, jnp.transpose(gcols, (1, 0, 2)), gtile

    return jax.shard_map(
        shards,
        mesh=mesh,
        in_specs=(
            P("ia", "ja", None),
            P("ja", "ia", None),
            P("ia", "ja", None),
            P("ia", "ja", None),
        )
        + (P(),) * 8,
        out_specs=(
            P("ia", "ja", None),
            P("ia", "ja", None),
            P("ja", "ia", None),
            P("ia", "ja", None),
        ),
        check_vma=False,
    )
```

```python
import functools
import math

import jax
import jax.numpy as jnp
from jax import lax
from jax.experimental import pallas as pl
from jax.experimental.pallas import tpu as pltpu
from jax.sharding import PartitionSpec as P

EPSILON = 1e-05
VMEM_BYTES = 56 * 1024 * 1024
MESH = pl.DeviceIdType.MESH
F32 = jnp.float32
BF16 = jnp.bfloat16


def chunk_of(count, rows, most):
    return max(d for d in range(1, count + 1) if count % d == 0 and (d * rows <= most or d == 1))


def normalize(values):
    centre = jnp.mean(values, axis=-1, keepdims=True)
    shifted = values - centre
    inverse = lax.rsqrt(jnp.mean(shifted * shifted, axis=-1, keepdims=True) + EPSILON)
    return shifted * inverse, inverse


def norm_back(scaled, inverse, grad_out, gain):
    grad_hat = grad_out * gain
    first_mean = jnp.mean(grad_hat, axis=-1, keepdims=True)
    second_mean = jnp.mean(grad_hat * scaled, axis=-1, keepdims=True)
    return inverse * (grad_hat - first_mean - scaled * second_mean)


def dot(a, b):
    return jnp.dot(a, b, preferred_element_type=F32)


def dot_t(a, b):
    return lax.dot_general(a, b, (((1,), (1,)), ((), ())), preferred_element_type=F32)


def kernel(
    n_ia,
    n_ja,
    slab_hbm,
    cols_hbm,
    tile_hbm,
    cot_hbm,
    wl_hbm,
    wr_hbm,
    wg_hbm,
    wo_hbm,
    gain_hbm,
    bias_hbm,
    ugain_hbm,
    ubias_hbm,
    update_ref,
    gslab_ref,
    gcols_ref,
    gtile_ref,
    slab_ref,
    cols_ref,
    tile_ref,
    cot_ref,
    wl_ref,
    wr_ref,
    wg_ref,
    wo_ref,
    gain_ref,
    bias_ref,
    ugain_ref,
    ubias_ref,
    in_sem,
    xs_l,
    save_l,
    save_r,
    left_all,
    right_all,
    left_f,
    right_f,
    dl_recv,
    dr_recv,
    tri_t,
    dtri,
    save_t,
    lsend,
    lrecv,
    rsend,
    rrecv,
    fsend,
    frecv,
    dlsend,
    dlrecv,
    drsend,
    drrecv,
    sibsend,
    sibrecv,
):
    my_ia, my_ja = lax.axis_index("ia"), lax.axis_index("ja")
    rows_i, k_l, ch = slab_ref.shape
    k_r, rows_j, _ = cols_ref.shape

    ins = [
        pltpu.make_async_copy(a, b, in_sem.at[n])
        for n, (a, b) in enumerate(
            [
                (cols_hbm, cols_ref),
                (wr_hbm, wr_ref),
                (gain_hbm, gain_ref),
                (bias_hbm, bias_ref),
                (slab_hbm, slab_ref),
                (wl_hbm, wl_ref),
                (tile_hbm, tile_ref),
                (wg_hbm, wg_ref),
                (cot_hbm, cot_ref),
                (wo_hbm, wo_ref),
                (ugain_hbm, ugain_ref),
                (ubias_hbm, ubias_ref),
            ]
        )
    ]
    for copy in ins:
        copy.start()

    n_z = n_ia // 2
    my_z, my_core = my_ia // 2, lax.rem(my_ia, 2)
    sibling = my_z * 2 + 1 - my_core
    square = n_ja == 4 and k_l % 4 == 0
    quarter = k_l // 4

    def ja_peer(s):
        if square:
            return lax.rem(my_ja // 2 + s // 2, 2) * 2 + lax.rem(my_ja + s, 2)
        return lax.rem(my_ja + s, n_ja)

    def ia_peer(s):
        return lax.rem(my_ia + s, n_ia)

    def z_peer(s):
        return lax.rem(my_z + s, n_z)

    barrier = pltpu.get_barrier_semaphore()

    def greet_ja(s, c):
        pl.semaphore_signal(barrier, inc=1, device_id=(my_ia, ja_peer(s)), device_id_type=MESH)
        return c

    def greet_ia(s, c):
        pl.semaphore_signal(barrier, inc=1, device_id=(ia_peer(s), my_ja), device_id_type=MESH)
        return c

    lax.fori_loop(1, n_ja, greet_ja, 0)
    lax.fori_loop(1, n_ia, greet_ia, 0)

    for copy in ins[:4]:
        copy.wait()
    gain = gain_ref[...]
    bias = bias_ref[...]
    pitch = xs_l.shape[0] // rows_i

    def slab_piece(k0, step):
        return jnp.concatenate(
            [xs_l[pl.ds(k0 + u, rows_i, stride=pitch), :] for u in range(step)], axis=0
        )

    def cols_piece(k0, step):
        return cols_ref[pl.ds(k0, step)].astype(F32).reshape(step * rows_j, ch)

    def project(piece, rows, start, count, w_ref, save, edges, base):
        step = chunk_of(count, rows, 256)

        def body(t, c):
            k0 = start + t * step
            x = piece(k0, step)
            scaled, inverse = normalize(x)
            q = dot((scaled * gain + bias).astype(BF16), w_ref[...])
            linear = q[:, :ch]
            sigma = jax.nn.sigmoid(q[:, ch:])
            at = pl.ds(pl.multiple_of(k0 * rows, 8), step * rows)
            save[0, at, :] = scaled
            save[1, at, :] = jnp.broadcast_to(inverse, scaled.shape)
            save[2, at, :] = linear
            save[3, at, :] = sigma
            edge = (sigma * linear).astype(BF16)
            edges[pl.ds(base + k0, step)] = edge.reshape(step, rows, ch)
            return c

        lax.fori_loop(0, count // step, body, 0)

    def left_copy(s):
        own = left_all.at[pl.ds(my_ja * k_l, k_l)]
        return pltpu.make_async_remote_copy(
            src_ref=own,
            dst_ref=own,
            send_sem=lsend.at[s],
            recv_sem=lrecv.at[s],
            device_id=(my_ia, ja_peer(s)),
            device_id_type=MESH,
        )

    def left_hop(owner, q, to, sem):
        piece = left_all.at[pl.ds(ja_peer(owner) * k_l + q * quarter, quarter)]
        return pltpu.make_async_remote_copy(
            src_ref=piece,
            dst_ref=piece,
            send_sem=lsend.at[sem],
            recv_sem=lrecv.at[sem],
            device_id=(my_ia, ja_peer(to)),
            device_id_type=MESH,
        )

    def own_hop(to, q):
        return left_hop(0, q, to, (to - 1) * 4 + q)

    relays = [left_hop(2 - (q + 1) % 2, q, 2 - q % 2, 8 + q) for q in range(4 * square)]

    def right_copy(s):
        own = right_all.at[pl.ds(my_ia * k_r, k_r)]
        return pltpu.make_async_remote_copy(
            src_ref=own,
            dst_ref=own,
            send_sem=rsend.at[s],
            recv_sem=rrecv.at[s],
            device_id=(z_peer(s) * 2 + my_core, my_ja),
            device_id_type=MESH,
        )

    def right_forward(s):
        piece = right_all.at[pl.ds((z_peer(n_z - s) * 2 + my_core) * k_r, k_r)]
        return pltpu.make_async_remote_copy(
            src_ref=piece,
            dst_ref=piece,
            send_sem=fsend.at[s],
            recv_sem=frecv.at[s],
            device_id=(sibling, my_ja),
            device_id_type=MESH,
        )

    def dl_copy(s):
        to = ja_peer(s)
        return pltpu.make_async_remote_copy(
            src_ref=left_all.at[pl.ds(to * k_l, k_l)],
            dst_ref=dl_recv.at[s],
            send_sem=dlsend.at[s],
            recv_sem=dlrecv.at[s],
            device_id=(my_ia, to),
            device_id_type=MESH,
        )

    def dl_hop(piece, q, to, slot, sem):
        return pltpu.make_async_remote_copy(
            src_ref=left_all.at[pl.ds(ja_peer(piece) * k_l + q * quarter, quarter)],
            dst_ref=dl_recv.at[slot, pl.ds(q * quarter, quarter)],
            send_sem=dlsend.at[sem],
            recv_sem=dlrecv.at[sem],
            device_id=(my_ia, ja_peer(to)),
            device_id_type=MESH,
        )

    def across_hop(q):
        return dl_hop(3, q, 1 + q % 2, 3, q)

    def near_hop(to, q):
        return dl_hop(to, q, to, to, to * 4 + q)

    def dr_sibling(s):
        return pltpu.make_async_remote_copy(
            src_ref=right_all.at[pl.ds((z_peer(s) * 2 + 1 - my_core) * k_r, k_r)],
            dst_ref=dr_recv.at[n_z + s],
            send_sem=sibsend.at[s],
            recv_sem=sibrecv.at[s],
            device_id=(sibling, my_ja),
            device_id_type=MESH,
        )

    def dr_copy(s):
        to = z_peer(s) * 2 + my_core
        return pltpu.make_async_remote_copy(
            src_ref=right_all.at[pl.ds(to * k_r, k_r)],
            dst_ref=dr_recv.at[s],
            send_sem=drsend.at[s],
            recv_sem=drrecv.at[s],
            device_id=(to, my_ja),
            device_id_type=MESH,
        )

    def each(copy, n, act):
        def body(s, c):
            act(copy(s))
            return c

        lax.fori_loop(1, n, body, 0)

    project(cols_piece, rows_j, 0, k_r, wr_ref, save_r, right_all, my_ia * k_r)
    pl.semaphore_wait(barrier, n_ia + n_ja - 2)
    each(right_copy, n_z, lambda c: c.start())
    right_forward(0).start()
    for copy in ins[4:6]:
        copy.wait()

    def widen(r, c):
        xs_l[pl.ds(pl.multiple_of(r * pitch, 8), k_l), :] = slab_ref[r].astype(F32)
        return c

    lax.fori_loop(0, rows_i, widen, 0, unroll=4)
    def project_slab(start, count):
        project(slab_piece, rows_i, start, count, wl_ref, save_l, left_all, my_ja * k_l)

    if square:

        def send_quarter(q, c):
            project_slab(q * quarter, quarter)
            own_hop(1, q).start()
            own_hop(2, q).start()
            return c

        lax.fori_loop(0, 4, send_quarter, 0)
    else:
        project_slab(0, k_l)
        each(left_copy, n_ja, lambda c: c.start())

    for copy in ins[6:]:
        copy.wait()
    ugain = ugain_ref[...]
    ubias = ubias_ref[...]
    t_rows = chunk_of(rows_i, rows_j, 128)
    t_flat = t_rows * rows_j

    def tile_slot(t):
        return pl.ds(pl.multiple_of(t * t_flat, 8), t_flat)

    def gate_body(t, c):
        x = tile_ref[pl.ds(t * t_rows, t_rows)].astype(F32).reshape(t_flat, ch)
        scaled, inverse = normalize(x)
        gate = jax.nn.sigmoid(dot((scaled * gain + bias).astype(BF16), wg_ref[...]))
        at = tile_slot(t)
        save_t[0, at, :] = scaled
        save_t[1, at, :] = jnp.broadcast_to(inverse, scaled.shape)
        save_t[2, at, :] = gate
        return c

    lax.fori_loop(0, rows_i // t_rows, gate_body, 0)

    def pass_on(s, c):
        right_copy(s).wait_recv()
        right_forward(s).start()
        return c

    def relay(q):
        own_hop(2 - (q + 1) % 2, q).wait_recv()
        relays[q].start()

    if square:
        relay(0)
        relay(1)
    lax.fori_loop(1, n_z, pass_on, 0)
    if square:
        relay(2)
        relay(3)
    each(right_copy, n_z, lambda c: c.wait_send())
    lax.fori_loop(0, n_z, lambda s, c: (right_forward(s).wait(), c)[1], 0)

    block = math.gcd(rows_j, 8)

    def tri_chunk(s, c):
        if square:

            @pl.when(s == 1)
            def _():
                own_hop(1, 1).wait_recv()
                own_hop(1, 3).wait_recv()

            @pl.when(s == 2)
            def _():
                own_hop(2, 0).wait_recv()
                own_hop(2, 2).wait_recv()

            @pl.when(s == 3)
            def _():
                for copy in relays:
                    copy.wait_recv()

            k_first = ja_peer(s) * k_l
        else:

            @pl.when(s > 0)
            def _():
                left_copy(s).wait()

            k_first = ja_peer(n_ja - s) * k_l

        def to_f32(k, c):
            left_f[k] = left_all[k].astype(F32)
            right_f[k] = right_all[k].astype(F32)
            return c

        lax.fori_loop(k_first, k_first + k_l, to_f32, 0)
        for first in range(0, rows_j, block):

            def tri_body(k, accs, first=first):
                l = left_f[k_first + k]
                return tuple(
                    acc + right_f[k_first + k, pl.ds(first + j, 1), :] * l
                    for j, acc in enumerate(accs)
                )

            accs = tuple(tri_t[pl.ds((first + j) * rows_i, rows_i), :] for j in range(block))
            accs = lax.fori_loop(0, k_l, tri_body, accs, unroll=2)
            for j, acc in enumerate(accs):
                tri_t[pl.ds((first + j) * rows_i, rows_i), :] = acc
        return c

    tri_t[...] = jnp.zeros_like(tri_t)
    lax.fori_loop(0, n_ja, tri_chunk, 0)
    if square:
        for q in range(4):
            own_hop(1, q).wait_send()
            own_hop(2, q).wait_send()
            relays[q].wait_send()

    def tile_body(t, c):
        at = tile_slot(t)
        tri = jnp.concatenate(
            [tri_t[pl.ds(t * t_rows + u, rows_j, stride=rows_i), :] for u in range(t_rows)], axis=0
        )
        scaled, inverse = normalize(tri)
        outer = dot((scaled * ugain + ubias).astype(BF16), wo_ref[...])
        gate = save_t[2, at, :]
        update_ref[pl.ds(t * t_rows, t_rows)] = (
            (gate * outer).astype(BF16).reshape(t_rows, rows_j, ch)
        )
        cot = cot_ref[pl.ds(t * t_rows, t_rows)].astype(F32).reshape(t_flat, ch)
        d_outer = (cot * gate).astype(BF16)
        save_t[3, at, :] = cot * outer * gate * (1.0 - gate)
        d_tri = norm_back(scaled, inverse, dot_t(d_outer, wo_ref[...]), ugain)
        d_tri = d_tri.astype(BF16).astype(F32)
        dtri[at, :] = d_tri
        for u in range(t_rows):
            tri_t[pl.ds(t * t_rows + u, rows_j, stride=rows_i), :] = d_tri[
                u * rows_j : (u + 1) * rows_j
            ]
        return c

    lax.fori_loop(0, rows_i // t_rows, tile_body, 0)

    def left_part(s, start=0, count=k_l):
        k_first = ja_peer(s) * k_l + start
        u_l = chunk_of(count, 1, 4)

        def body(t, c):
            k0 = k_first + t * u_l
            accs = [None] * u_l
            for j in range(rows_j):
                d = tri_t[pl.ds(j * rows_i, rows_i), :]
                for u in range(u_l):
                    term = right_f[k0 + u, pl.ds(j, 1), :] * d
                    accs[u] = term if j == 0 else accs[u] + term
            for u in range(u_l):
                left_all[k0 + u] = accs[u].astype(BF16)
            return c

        lax.fori_loop(0, count // u_l, body, 0)

    def right_part(to, came=None):
        k_first = to * k_r
        u_r = math.gcd(k_r, 4)

        def body(t, c):
            k0 = k_first + t * u_r
            accs = [None] * u_r
            for i in range(rows_i):
                d = dtri[pl.ds(i * rows_j, rows_j), :]
                for u in range(u_r):
                    term = left_f[k0 + u, pl.ds(i, 1), :] * d
                    accs[u] = term if i == 0 else accs[u] + term
            for u in range(u_r):
                acc = accs[u]
                if came is not None:
                    acc = acc + dr_recv[came, t * u_r + u].astype(F32)
                right_all[k0 + u] = acc.astype(BF16)
            return c

        lax.fori_loop(0, k_r // u_r, body, 0)

    def for_sibling(v, c):
        s = lax.rem(v + 1, n_z)
        right_part(z_peer(s) * 2 + 1 - my_core)
        dr_sibling(s).start()
        return c

    def for_core(s, c):
        dr_sibling(s).wait_recv()
        right_part(z_peer(s) * 2 + my_core, n_z + s)
        dr_copy(s).start()
        return c

    def for_ja(s, c):
        left_part(s)
        dl_copy(s).start()
        return c

    def across(q, c):
        left_part(3, q * quarter, quarter)
        across_hop(q).start()
        return c

    def add_across(q):
        across_hop(q).wait_recv()
        to = 2 - q % 2
        at = pl.ds(ja_peer(to) * k_l + q * quarter, quarter)
        came = dl_recv[3, pl.ds(q * quarter, quarter)].astype(F32)
        left_all[at] = (left_all[at].astype(F32) + came).astype(BF16)
        near_hop(to, q).start()

    if square:
        lax.fori_loop(0, 4, across, 0)
        lax.fori_loop(0, n_z, for_sibling, 0)
        left_part(1)
        near_hop(1, 0).start()
        near_hop(1, 2).start()
        left_part(2)
        near_hop(2, 1).start()
        near_hop(2, 3).start()
        lax.fori_loop(1, n_z, for_core, 0)
        for q in range(4):
            add_across(q)
    else:
        lax.fori_loop(0, n_z, for_sibling, 0)
        lax.fori_loop(1, n_z, for_core, 0)
        lax.fori_loop(1, n_ja, for_ja, 0)
    left_part(0)
    dr_sibling(0).wait_recv()
    right_part(my_ia)

    def tile_back(t, c):
        at = tile_slot(t)
        grad = dot_t(save_t[3, at, :].astype(BF16), wg_ref[...])
        out = norm_back(save_t[0, at, :], save_t[1, at, :], grad, gain)
        gtile_ref[pl.ds(t * t_rows, t_rows)] = out.astype(BF16).reshape(t_rows, rows_j, ch)
        return c

    lax.fori_loop(0, rows_i // t_rows, tile_back, 0)

    def project_back(put, rows, start, count, w_ref, save, edges, base, recv, first, n):
        step = chunk_of(count, rows, 256)

        def body(t, c):
            k0 = start + t * step
            at = pl.ds(pl.multiple_of(k0 * rows, 8), step * rows)
            d = edges[pl.ds(base + k0, step)].astype(F32)

            def add(s, d):
                return d + recv[s, pl.ds(k0, step)].astype(F32)

            d = lax.fori_loop(first, n, add, d, unroll=n <= 8).reshape(step * rows, ch)
            linear, sigma = save[2, at, :], save[3, at, :]
            p = jnp.concatenate([d * sigma, d * linear * sigma * (1.0 - sigma)], axis=-1)
            grad = dot_t(p.astype(BF16), w_ref[...])
            put(k0, step, norm_back(save[0, at, :], save[1, at, :], grad, gain))
            return c

        lax.fori_loop(0, count // step, body, 0)

    def put_cols(k0, step, out):
        gcols_ref[pl.ds(k0, step)] = out.astype(BF16).reshape(step, rows_j, ch)

    def put_slab(k0, step, out):
        for u in range(step):
            xs_l[pl.ds(k0 + u, rows_i, stride=pitch), :] = out[u * rows_i : (u + 1) * rows_i]

    each(dr_copy, n_z, lambda c: c.wait())
    lax.fori_loop(0, n_z, lambda s, c: (dr_sibling(s).wait_send(), c)[1], 0)
    project_back(
        put_cols, rows_j, 0, k_r, wr_ref, save_r, right_all, my_ia * k_r, dr_recv, 1, n_z + 1
    )
    def back_slab(start, count, last):
        project_back(
            put_slab, rows_i, start, count, wl_ref, save_l, left_all, my_ja * k_l, dl_recv, 1, last
        )

    if square:

        def back_quarter(q, c):
            near_hop(1, q).wait_recv()
            near_hop(2, q).wait_recv()
            back_slab(q * quarter, quarter, 3)
            return c

        lax.fori_loop(0, 4, back_quarter, 0)
        for q in range(4):
            across_hop(q).wait_send()
            near_hop(1, q).wait_send()
            near_hop(2, q).wait_send()
    else:
        each(dl_copy, n_ja, lambda c: c.wait())
        back_slab(0, k_l, n_ja)

    def narrow(r, c):
        gslab_ref[r] = xs_l[pl.ds(pl.multiple_of(r * pitch, 8), k_l), :].astype(BF16)
        return c

    lax.fori_loop(0, rows_i, narrow, 0, unroll=4)


def move(*refs):
    n = len(refs) // 2
    copies = [pltpu.make_async_copy(refs[m], refs[n + m], refs[-1].at[m]) for m in range(n)]
    for copy in copies:
        copy.start()
    for copy in copies:
        copy.wait()


def solution(mesh):
    n_ia, n_ja = mesh.shape["ia"], mesh.shape["ja"]

    def shards(slab, cols, tile, cot, wl, wr, wg, wo, gain, bias, ugain, ubias):
        cols = jnp.transpose(cols, (1, 0, 2))
        rows_i, k_l, ch = slab.shape
        k_r, rows_j, _ = cols.shape
        res = k_l * n_ja
        pitch = -(-k_l // 8) * 8
        anywhere = pl.BlockSpec(memory_space=pl.ANY)
        flat = rows_i * rows_j
        dma = pltpu.SemaphoreType.DMA
        ins = (
            slab, cols, tile, cot, wl, wr, wg, wo,
            gain[None, :], bias[None, :], ugain[None, :], ubias[None, :],
        )
        results = [jax.ShapeDtypeStruct(a.shape, BF16) for a in (tile, slab, cols, tile)]
        buffers = (
            [(a.shape, a.dtype) for a in ins]
            + [
                ((rows_i * pitch, ch), F32),
                ((4, rows_i * k_l, ch), F32),
                ((4, rows_j * k_r, ch), F32),
                ((res, rows_i, ch), BF16),
                ((res, rows_j, ch), BF16),
                ((res, rows_i, ch), F32),
                ((res, rows_j, ch), F32),
                ((n_ja, k_l, rows_i, ch), BF16),
                ((n_ia, k_r, rows_j, ch), BF16),
                ((flat, ch), F32),
                ((flat, ch), F32),
                ((4, flat, ch), F32),
            ]
        )
        scratch = [pltpu.VMEM(shape, kind) for shape, kind in buffers]
        vmem = pl.BlockSpec(memory_space=pltpu.VMEM)
        done = pl.pallas_call(
            functools.partial(kernel, n_ia, n_ja),
            out_shape=[pltpu.VMEM(a.shape, a.dtype) for a in results],
            in_specs=[pl.BlockSpec(memory_space=pltpu.HBM)] * len(ins),
            out_specs=[vmem] * len(results),
            scratch_shapes=scratch[: len(ins)]
            + [dma((len(ins),))]
            + scratch[len(ins) :]
            + [dma((n,)) for n in (n_ja + 8, n_ja + 8, n_ia, n_ia, n_ia, n_ia) * 2],
            compiler_params=pltpu.CompilerParams(
                collective_id=0, has_side_effects=True, vmem_limit_bytes=VMEM_BYTES
            ),
        )(*ins)
        update, gslab, gcols, gtile = pl.pallas_call(
            move,
            out_shape=results,
            in_specs=[vmem] * len(results),
            out_specs=[anywhere] * len(results),
            scratch_shapes=[dma((len(results),))],
            compiler_params=pltpu.CompilerParams(vmem_limit_bytes=VMEM_BYTES),
        )(*[pltpu.with_memory_space_constraint(a, pltpu.VMEM) for a in done])
        return update, gslab, jnp.transpose(gcols, (1, 0, 2)), gtile

    return jax.shard_map(
        shards,
        mesh=mesh,
        in_specs=(
            P("ia", "ja", None),
            P("ja", "ia", None),
            P("ia", "ja", None),
            P("ia", "ja", None),
        )
        + (P(),) * 8,
        out_specs=(
            P("ia", "ja", None),
            P("ia", "ja", None),
            P("ja", "ia", None),
            P("ia", "ja", None),
        ),
        check_vma=False,
    )
```

```python
import functools
import math

import jax
import jax.numpy as jnp
from jax import lax
from jax.experimental import pallas as pl
from jax.experimental.pallas import tpu as pltpu
from jax.sharding import PartitionSpec as P

EPSILON = 1e-05
VMEM_BYTES = 56 * 1024 * 1024
MESH = pl.DeviceIdType.MESH
F32 = jnp.float32
BF16 = jnp.bfloat16


def chunk_of(count, rows, most):
    return max(d for d in range(1, count + 1) if count % d == 0 and (d * rows <= most or d == 1))


def normalize(values):
    centre = jnp.mean(values, axis=-1, keepdims=True)
    shifted = values - centre
    inverse = lax.rsqrt(jnp.mean(shifted * shifted, axis=-1, keepdims=True) + EPSILON)
    return shifted * inverse, inverse


def norm_back(scaled, inverse, grad_out, gain):
    grad_hat = grad_out * gain
    first_mean = jnp.mean(grad_hat, axis=-1, keepdims=True)
    second_mean = jnp.mean(grad_hat * scaled, axis=-1, keepdims=True)
    return inverse * (grad_hat - first_mean - scaled * second_mean)


def dot(a, b):
    return jnp.dot(a, b, preferred_element_type=F32)


def dot_t(a, b):
    return lax.dot_general(a, b, (((1,), (1,)), ((), ())), preferred_element_type=F32)


def kernel(
    n_ia,
    n_ja,
    slab_hbm,
    cols_hbm,
    tile_hbm,
    cot_hbm,
    wl_hbm,
    wr_hbm,
    wg_hbm,
    wo_hbm,
    gain_hbm,
    bias_hbm,
    ugain_hbm,
    ubias_hbm,
    update_ref,
    gslab_ref,
    gcols_ref,
    gtile_ref,
    slab_ref,
    cols_ref,
    tile_ref,
    cot_ref,
    wl_ref,
    wr_ref,
    wg_ref,
    wo_ref,
    gain_ref,
    bias_ref,
    ugain_ref,
    ubias_ref,
    in_sem,
    xs_l,
    save_l,
    save_r,
    left_all,
    right_all,
    left_f,
    right_f,
    dl_recv,
    dr_recv,
    tri_t,
    dtri,
    save_t,
    lsend,
    lrecv,
    rsend,
    rrecv,
    fsend,
    frecv,
    dlsend,
    dlrecv,
    drsend,
    drrecv,
    sibsend,
    sibrecv,
):
    my_ia, my_ja = lax.axis_index("ia"), lax.axis_index("ja")
    rows_i, k_l, ch = slab_ref.shape
    k_r, rows_j, _ = cols_ref.shape

    ins = [
        pltpu.make_async_copy(a, b, in_sem.at[n])
        for n, (a, b) in enumerate(
            [
                (cols_hbm, cols_ref),
                (wr_hbm, wr_ref),
                (gain_hbm, gain_ref),
                (bias_hbm, bias_ref),
                (slab_hbm, slab_ref),
                (wl_hbm, wl_ref),
                (tile_hbm, tile_ref),
                (wg_hbm, wg_ref),
                (cot_hbm, cot_ref),
                (wo_hbm, wo_ref),
                (ugain_hbm, ugain_ref),
                (ubias_hbm, ubias_ref),
            ]
        )
    ]
    for copy in ins:
        copy.start()

    n_z = n_ia // 2
    my_z, my_core = my_ia // 2, lax.rem(my_ia, 2)
    sibling = my_z * 2 + 1 - my_core
    square = n_ja == 4 and k_l % 4 == 0
    quarter = k_l // 4

    def ja_peer(s):
        if square:
            return lax.rem(my_ja // 2 + s // 2, 2) * 2 + lax.rem(my_ja + s, 2)
        return lax.rem(my_ja + s, n_ja)

    def ia_peer(s):
        return lax.rem(my_ia + s, n_ia)

    def z_peer(s):
        return lax.rem(my_z + s, n_z)

    barrier = pltpu.get_barrier_semaphore()

    def greet_ja(s, c):
        pl.semaphore_signal(barrier, inc=1, device_id=(my_ia, ja_peer(s)), device_id_type=MESH)
        return c

    def greet_ia(s, c):
        pl.semaphore_signal(barrier, inc=1, device_id=(ia_peer(s), my_ja), device_id_type=MESH)
        return c

    lax.fori_loop(1, n_ja, greet_ja, 0)
    lax.fori_loop(1, n_ia, greet_ia, 0)

    for copy in ins[:4]:
        copy.wait()
    gain = gain_ref[...]
    bias = bias_ref[...]
    pitch = xs_l.shape[0] // rows_i

    def slab_piece(k0, step):
        return jnp.concatenate(
            [xs_l[pl.ds(k0 + u, rows_i, stride=pitch), :] for u in range(step)], axis=0
        )

    def cols_piece(k0, step):
        return cols_ref[pl.ds(k0, step)].astype(F32).reshape(step * rows_j, ch)

    def project(piece, rows, start, count, w_ref, save, edges, base):
        step = chunk_of(count, rows, 256)

        def body(t, c):
            k0 = start + t * step
            x = piece(k0, step)
            scaled, inverse = normalize(x)
            q = dot((scaled * gain + bias).astype(BF16), w_ref[...])
            linear = q[:, :ch]
            sigma = jax.nn.sigmoid(q[:, ch:])
            at = pl.ds(pl.multiple_of(k0 * rows, 8), step * rows)
            save[0, at, :] = scaled
            save[1, at, :] = jnp.broadcast_to(inverse, scaled.shape)
            save[2, at, :] = linear
            save[3, at, :] = sigma
            edge = (sigma * linear).astype(BF16)
            edges[pl.ds(base + k0, step)] = edge.reshape(step, rows, ch)
            return c

        lax.fori_loop(0, count // step, body, 0)

    def left_copy(s):
        own = left_all.at[pl.ds(my_ja * k_l, k_l)]
        return pltpu.make_async_remote_copy(
            src_ref=own,
            dst_ref=own,
            send_sem=lsend.at[s],
            recv_sem=lrecv.at[s],
            device_id=(my_ia, ja_peer(s)),
            device_id_type=MESH,
        )

    def left_hop(owner, q, to, sem):
        piece = left_all.at[pl.ds(ja_peer(owner) * k_l + q * quarter, quarter)]
        return pltpu.make_async_remote_copy(
            src_ref=piece,
            dst_ref=piece,
            send_sem=lsend.at[sem],
            recv_sem=lrecv.at[sem],
            device_id=(my_ia, ja_peer(to)),
            device_id_type=MESH,
        )

    def own_hop(to, q):
        return left_hop(0, q, to, (to - 1) * 4 + q)

    relays = [left_hop(2 - (q + 1) % 2, q, 2 - q % 2, 8 + q) for q in range(4 * square)]

    def right_copy(s):
        own = right_all.at[pl.ds(my_ia * k_r, k_r)]
        return pltpu.make_async_remote_copy(
            src_ref=own,
            dst_ref=own,
            send_sem=rsend.at[s],
            recv_sem=rrecv.at[s],
            device_id=(z_peer(s) * 2 + my_core, my_ja),
            device_id_type=MESH,
        )

    def right_forward(s):
        piece = right_all.at[pl.ds((z_peer(n_z - s) * 2 + my_core) * k_r, k_r)]
        return pltpu.make_async_remote_copy(
            src_ref=piece,
            dst_ref=piece,
            send_sem=fsend.at[s],
            recv_sem=frecv.at[s],
            device_id=(sibling, my_ja),
            device_id_type=MESH,
        )

    def dl_copy(s):
        to = ja_peer(s)
        return pltpu.make_async_remote_copy(
            src_ref=left_all.at[pl.ds(to * k_l, k_l)],
            dst_ref=dl_recv.at[s],
            send_sem=dlsend.at[s],
            recv_sem=dlrecv.at[s],
            device_id=(my_ia, to),
            device_id_type=MESH,
        )

    def dl_hop(piece, q, to, slot, sem):
        return pltpu.make_async_remote_copy(
            src_ref=left_all.at[pl.ds(ja_peer(piece) * k_l + q * quarter, quarter)],
            dst_ref=dl_recv.at[slot, pl.ds(q * quarter, quarter)],
            send_sem=dlsend.at[sem],
            recv_sem=dlrecv.at[sem],
            device_id=(my_ia, ja_peer(to)),
            device_id_type=MESH,
        )

    def across_hop(q):
        return dl_hop(3, q, 1 + q % 2, 3, q)

    def near_hop(to, q):
        return dl_hop(to, q, to, to, to * 4 + q)

    def dr_sibling(s):
        return pltpu.make_async_remote_copy(
            src_ref=right_all.at[pl.ds((z_peer(s) * 2 + 1 - my_core) * k_r, k_r)],
            dst_ref=dr_recv.at[n_z + s],
            send_sem=sibsend.at[s],
            recv_sem=sibrecv.at[s],
            device_id=(sibling, my_ja),
            device_id_type=MESH,
        )

    def dr_copy(s):
        to = z_peer(s) * 2 + my_core
        return pltpu.make_async_remote_copy(
            src_ref=right_all.at[pl.ds(to * k_r, k_r)],
            dst_ref=dr_recv.at[s],
            send_sem=drsend.at[s],
            recv_sem=drrecv.at[s],
            device_id=(to, my_ja),
            device_id_type=MESH,
        )

    def each(copy, n, act):
        def body(s, c):
            act(copy(s))
            return c

        lax.fori_loop(1, n, body, 0)

    project(cols_piece, rows_j, 0, k_r, wr_ref, save_r, right_all, my_ia * k_r)
    pl.semaphore_wait(barrier, n_ia + n_ja - 2)
    each(right_copy, n_z, lambda c: c.start())
    right_forward(0).start()
    for copy in ins[4:6]:
        copy.wait()

    def widen(r, c):
        xs_l[pl.ds(pl.multiple_of(r * pitch, 8), k_l), :] = slab_ref[r].astype(F32)
        return c

    lax.fori_loop(0, rows_i, widen, 0, unroll=4)
    def project_slab(start, count):
        project(slab_piece, rows_i, start, count, wl_ref, save_l, left_all, my_ja * k_l)

    if square:

        def send_quarter(q, c):
            project_slab(q * quarter, quarter)
            own_hop(1, q).start()
            own_hop(2, q).start()
            return c

        lax.fori_loop(0, 4, send_quarter, 0)
    else:
        project_slab(0, k_l)
        each(left_copy, n_ja, lambda c: c.start())

    def pass_on(s, c):
        right_copy(s).wait_recv()
        right_forward(s).start()
        return c

    def relay(q):
        own_hop(2 - (q + 1) % 2, q).wait_recv()
        relays[q].start()

    if square:
        relay(0)

    for copy in ins[6:]:
        copy.wait()
    ugain = ugain_ref[...]
    ubias = ubias_ref[...]
    t_rows = chunk_of(rows_i, rows_j, 512)
    t_flat = t_rows * rows_j

    def by_j(i):
        return pl.ds(i, rows_j, stride=rows_i)

    def gate_body(t, c):
        x = tile_ref[pl.ds(t * t_rows, t_rows)].astype(F32).reshape(t_flat, ch)
        scaled, inverse = normalize(x)
        gate = jax.nn.sigmoid(dot((scaled * gain + bias).astype(BF16), wg_ref[...]))
        at = pl.ds(pl.multiple_of(t * t_flat, 8), t_flat)
        save_t[0, at, :] = scaled
        save_t[1, at, :] = jnp.broadcast_to(inverse, scaled.shape)
        for u in range(t_rows):
            save_t[2, by_j(t * t_rows + u), :] = gate[u * rows_j : (u + 1) * rows_j]
            save_t[3, by_j(t * t_rows + u), :] = cot_ref[t * t_rows + u].astype(F32)
        return c

    lax.fori_loop(0, rows_i // t_rows, gate_body, 0)

    if square:
        relay(1)
    lax.fori_loop(1, n_z, pass_on, 0)
    if square:
        relay(2)
        relay(3)
    each(right_copy, n_z, lambda c: c.wait_send())
    lax.fori_loop(0, n_z, lambda s, c: (right_forward(s).wait(), c)[1], 0)

    block = math.gcd(rows_j, 8)

    def tri_chunk(s, c):
        if square:

            @pl.when(s == 1)
            def _():
                own_hop(1, 1).wait_recv()
                own_hop(1, 3).wait_recv()

            @pl.when(s == 2)
            def _():
                own_hop(2, 0).wait_recv()
                own_hop(2, 2).wait_recv()

            @pl.when(s == 3)
            def _():
                for copy in relays:
                    copy.wait_recv()

            k_first = ja_peer(s) * k_l
        else:

            @pl.when(s > 0)
            def _():
                left_copy(s).wait()

            k_first = ja_peer(n_ja - s) * k_l

        def to_f32(k, c):
            left_f[k] = left_all[k].astype(F32)
            right_f[k] = right_all[k].astype(F32)
            return c

        lax.fori_loop(k_first, k_first + k_l, to_f32, 0)
        for first in range(0, rows_j, block):

            def tri_body(k, accs, first=first):
                l = left_f[k_first + k]
                return tuple(
                    acc + right_f[k_first + k, pl.ds(first + j, 1), :] * l
                    for j, acc in enumerate(accs)
                )

            accs = tuple(tri_t[pl.ds((first + j) * rows_i, rows_i), :] for j in range(block))
            accs = lax.fori_loop(0, k_l, tri_body, accs, unroll=2)
            for j, acc in enumerate(accs):
                tri_t[pl.ds((first + j) * rows_i, rows_i), :] = acc
        return c

    tri_t[...] = jnp.zeros_like(tri_t)
    lax.fori_loop(0, n_ja, tri_chunk, 0)
    if square:
        for q in range(4):
            own_hop(1, q).wait_send()
            own_hop(2, q).wait_send()
            relays[q].wait_send()

    j_rows = chunk_of(rows_j, rows_i, 512)

    def tile_body(t, c):
        at = pl.ds(pl.multiple_of(t * j_rows * rows_i, 8), j_rows * rows_i)
        scaled, inverse = normalize(tri_t[at, :])
        outer = dot((scaled * ugain + ubias).astype(BF16), wo_ref[...])
        gate, cot = save_t[2, at, :], save_t[3, at, :]
        d_outer = (cot * gate).astype(BF16)
        d_tri = norm_back(scaled, inverse, dot_t(d_outer, wo_ref[...]), ugain)
        tri_t[at, :] = d_tri.astype(BF16).astype(F32)
        update = gate * outer
        save_t[2, at, :] = update
        save_t[3, at, :] = cot * update * (1.0 - gate)
        return c

    lax.fori_loop(0, rows_j // j_rows, tile_body, 0)

    def left_part(s, start=0, count=k_l):
        k_first = ja_peer(s) * k_l + start
        u_l = chunk_of(count, 1, 4)

        def body(t, c):
            k0 = k_first + t * u_l
            accs = [None] * u_l
            for j in range(rows_j):
                d = tri_t[pl.ds(j * rows_i, rows_i), :]
                for u in range(u_l):
                    term = right_f[k0 + u, pl.ds(j, 1), :] * d
                    accs[u] = term if j == 0 else accs[u] + term
            for u in range(u_l):
                left_all[k0 + u] = accs[u].astype(BF16)
            return c

        lax.fori_loop(0, count // u_l, body, 0)

    def right_part(to, came=None):
        k_first = to * k_r
        u_r = math.gcd(k_r, 4)

        def body(t, c):
            k0 = k_first + t * u_r
            accs = [None] * u_r
            for i in range(rows_i):
                d = dtri[pl.ds(i * rows_j, rows_j), :]
                for u in range(u_r):
                    term = left_f[k0 + u, pl.ds(i, 1), :] * d
                    accs[u] = term if i == 0 else accs[u] + term
            for u in range(u_r):
                acc = accs[u]
                if came is not None:
                    acc = acc + dr_recv[came, t * u_r + u].astype(F32)
                right_all[k0 + u] = acc.astype(BF16)
            return c

        lax.fori_loop(0, k_r // u_r, body, 0)

    def for_sibling(v, c):
        s = lax.rem(v + 1, n_z)
        right_part(z_peer(s) * 2 + 1 - my_core)
        dr_sibling(s).start()
        return c

    def for_core(s, c):
        dr_sibling(s).wait_recv()
        right_part(z_peer(s) * 2 + my_core, n_z + s)
        dr_copy(s).start()
        return c

    def for_ja(s, c):
        left_part(s)
        dl_copy(s).start()
        return c

    def across(q, c):
        left_part(3, q * quarter, quarter)
        across_hop(q).start()
        return c

    def add_across(q):
        across_hop(q).wait_recv()
        to = 2 - q % 2
        at = pl.ds(ja_peer(to) * k_l + q * quarter, quarter)
        came = dl_recv[3, pl.ds(q * quarter, quarter)].astype(F32)
        left_all[at] = (left_all[at].astype(F32) + came).astype(BF16)
        near_hop(to, q).start()

    def reorder(i, c):
        dtri[pl.ds(pl.multiple_of(i * rows_j, 8), rows_j), :] = tri_t[by_j(i), :]
        return c

    if square:
        lax.fori_loop(0, 4, across, 0)
        lax.fori_loop(0, rows_i, reorder, 0, unroll=8)
        lax.fori_loop(0, n_z, for_sibling, 0)
        left_part(1)
        near_hop(1, 0).start()
        near_hop(1, 2).start()
        left_part(2)
        near_hop(2, 1).start()
        near_hop(2, 3).start()
        lax.fori_loop(1, n_z, for_core, 0)
        for q in range(4):
            add_across(q)
    else:
        lax.fori_loop(0, rows_i, reorder, 0, unroll=8)
        lax.fori_loop(0, n_z, for_sibling, 0)
        lax.fori_loop(1, n_z, for_core, 0)
        lax.fori_loop(1, n_ja, for_ja, 0)
    left_part(0)
    dr_sibling(0).wait_recv()
    right_part(my_ia)

    def tile_back(t, c):
        at = pl.ds(pl.multiple_of(t * t_flat, 8), t_flat)
        first = t * t_rows
        for u in range(t_rows):
            update_ref[first + u] = save_t[2, by_j(first + u), :].astype(BF16)
        d_gate = jnp.concatenate([save_t[3, by_j(first + u), :] for u in range(t_rows)], axis=0)
        grad = dot_t(d_gate.astype(BF16), wg_ref[...])
        out = norm_back(save_t[0, at, :], save_t[1, at, :], grad, gain)
        gtile_ref[pl.ds(first, t_rows)] = out.astype(BF16).reshape(t_rows, rows_j, ch)
        return c

    lax.fori_loop(0, rows_i // t_rows, tile_back, 0)

    def project_back(put, rows, start, count, w_ref, save, edges, base, recv, first, n):
        step = chunk_of(count, rows, 512)

        def body(t, c):
            k0 = start + t * step
            at = pl.ds(pl.multiple_of(k0 * rows, 8), step * rows)
            d = edges[pl.ds(base + k0, step)].astype(F32)

            def add(s, d):
                return d + recv[s, pl.ds(k0, step)].astype(F32)

            d = lax.fori_loop(first, n, add, d, unroll=n <= 8).reshape(step * rows, ch)
            linear, sigma = save[2, at, :], save[3, at, :]
            p = jnp.concatenate([d * sigma, d * linear * sigma * (1.0 - sigma)], axis=-1)
            grad = dot_t(p.astype(BF16), w_ref[...])
            put(k0, step, norm_back(save[0, at, :], save[1, at, :], grad, gain))
            return c

        lax.fori_loop(0, count // step, body, 0)

    def put_cols(k0, step, out):
        gcols_ref[pl.ds(k0, step)] = out.astype(BF16).reshape(step, rows_j, ch)

    def put_slab(k0, step, out):
        for u in range(step):
            xs_l[pl.ds(k0 + u, rows_i, stride=pitch), :] = out[u * rows_i : (u + 1) * rows_i]

    each(dr_copy, n_z, lambda c: c.wait())
    lax.fori_loop(0, n_z, lambda s, c: (dr_sibling(s).wait_send(), c)[1], 0)
    project_back(
        put_cols, rows_j, 0, k_r, wr_ref, save_r, right_all, my_ia * k_r, dr_recv, 1, n_z + 1
    )
    def back_slab(start, count, last):
        project_back(
            put_slab, rows_i, start, count, wl_ref, save_l, left_all, my_ja * k_l, dl_recv, 1, last
        )

    if square:

        def back_half(h, c):
            for q in (h * 2, h * 2 + 1):
                near_hop(1, q).wait_recv()
                near_hop(2, q).wait_recv()
            back_slab(h * 2 * quarter, 2 * quarter, 3)
            return c

        lax.fori_loop(0, 2, back_half, 0)
        for q in range(4):
            across_hop(q).wait_send()
            near_hop(1, q).wait_send()
            near_hop(2, q).wait_send()
    else:
        each(dl_copy, n_ja, lambda c: c.wait())
        back_slab(0, k_l, n_ja)

    def narrow(r, c):
        gslab_ref[r] = xs_l[pl.ds(pl.multiple_of(r * pitch, 8), k_l), :].astype(BF16)
        return c

    lax.fori_loop(0, rows_i, narrow, 0, unroll=4)


def move(*refs):
    n = len(refs) // 2
    copies = [pltpu.make_async_copy(refs[m], refs[n + m], refs[-1].at[m]) for m in range(n)]
    for copy in copies:
        copy.start()
    for copy in copies:
        copy.wait()


def solution(mesh):
    n_ia, n_ja = mesh.shape["ia"], mesh.shape["ja"]

    def shards(slab, cols, tile, cot, wl, wr, wg, wo, gain, bias, ugain, ubias):
        cols = jnp.transpose(cols, (1, 0, 2))
        rows_i, k_l, ch = slab.shape
        k_r, rows_j, _ = cols.shape
        res = k_l * n_ja
        pitch = -(-k_l // 8) * 8
        anywhere = pl.BlockSpec(memory_space=pl.ANY)
        flat = rows_i * rows_j
        dma = pltpu.SemaphoreType.DMA
        ins = (
            slab, cols, tile, cot, wl, wr, wg, wo,
            gain[None, :], bias[None, :], ugain[None, :], ubias[None, :],
        )
        results = [jax.ShapeDtypeStruct(a.shape, BF16) for a in (tile, slab, cols, tile)]
        buffers = (
            [(a.shape, a.dtype) for a in ins]
            + [
                ((rows_i * pitch, ch), F32),
                ((4, rows_i * k_l, ch), F32),
                ((4, rows_j * k_r, ch), F32),
                ((res, rows_i, ch), BF16),
                ((res, rows_j, ch), BF16),
                ((res, rows_i, ch), F32),
                ((res, rows_j, ch), F32),
                ((n_ja, k_l, rows_i, ch), BF16),
                ((n_ia, k_r, rows_j, ch), BF16),
                ((flat, ch), F32),
                ((flat, ch), F32),
                ((4, flat, ch), F32),
            ]
        )
        scratch = [pltpu.VMEM(shape, kind) for shape, kind in buffers]
        vmem = pl.BlockSpec(memory_space=pltpu.VMEM)
        done = pl.pallas_call(
            functools.partial(kernel, n_ia, n_ja),
            out_shape=[pltpu.VMEM(a.shape, a.dtype) for a in results],
            in_specs=[pl.BlockSpec(memory_space=pltpu.HBM)] * len(ins),
            out_specs=[vmem] * len(results),
            scratch_shapes=scratch[: len(ins)]
            + [dma((len(ins),))]
            + scratch[len(ins) :]
            + [dma((n,)) for n in (n_ja + 8, n_ja + 8, n_ia, n_ia, n_ia, n_ia) * 2],
            compiler_params=pltpu.CompilerParams(
                collective_id=0, has_side_effects=True, vmem_limit_bytes=VMEM_BYTES
            ),
        )(*ins)
        update, gslab, gcols, gtile = pl.pallas_call(
            move,
            out_shape=results,
            in_specs=[vmem] * len(results),
            out_specs=[anywhere] * len(results),
            scratch_shapes=[dma((len(results),))],
            compiler_params=pltpu.CompilerParams(vmem_limit_bytes=VMEM_BYTES),
        )(*[pltpu.with_memory_space_constraint(a, pltpu.VMEM) for a in done])
        return update, gslab, jnp.transpose(gcols, (1, 0, 2)), gtile

    return jax.shard_map(
        shards,
        mesh=mesh,
        in_specs=(
            P("ia", "ja", None),
            P("ja", "ia", None),
            P("ia", "ja", None),
            P("ia", "ja", None),
        )
        + (P(),) * 8,
        out_specs=(
            P("ia", "ja", None),
            P("ia", "ja", None),
            P("ja", "ia", None),
            P("ia", "ja", None),
        ),
        check_vma=False,
    )
```

```python
import functools
import math

import jax
import jax.numpy as jnp
from jax import lax
from jax.experimental import pallas as pl
from jax.experimental.pallas import tpu as pltpu
from jax.sharding import PartitionSpec as P

EPSILON = 1e-05
VMEM_BYTES = 56 * 1024 * 1024
MESH = pl.DeviceIdType.MESH
F32 = jnp.float32
BF16 = jnp.bfloat16


def chunk_of(count, rows, most):
    return max(d for d in range(1, count + 1) if count % d == 0 and (d * rows <= most or d == 1))


def normalize(values):
    centre = jnp.mean(values, axis=-1, keepdims=True)
    shifted = values - centre
    inverse = lax.rsqrt(jnp.mean(shifted * shifted, axis=-1, keepdims=True) + EPSILON)
    return shifted * inverse, inverse


def norm_back(scaled, inverse, grad_out, gain):
    grad_hat = grad_out * gain
    first_mean = jnp.mean(grad_hat, axis=-1, keepdims=True)
    second_mean = jnp.mean(grad_hat * scaled, axis=-1, keepdims=True)
    return inverse * (grad_hat - first_mean - scaled * second_mean)


def dot(a, b):
    return jnp.dot(a, b, preferred_element_type=F32)


def dot_t(a, b):
    return lax.dot_general(a, b, (((1,), (1,)), ((), ())), preferred_element_type=F32)


def kernel(
    n_ia,
    n_ja,
    slab_hbm,
    cols_hbm,
    tile_hbm,
    cot_hbm,
    wl_hbm,
    wr_hbm,
    wg_hbm,
    wo_hbm,
    gain_hbm,
    bias_hbm,
    ugain_hbm,
    ubias_hbm,
    update_ref,
    gslab_ref,
    gcols_ref,
    gtile_ref,
    slab_ref,
    cols_ref,
    tile_ref,
    cot_ref,
    wl_ref,
    wr_ref,
    wg_ref,
    wo_ref,
    gain_ref,
    bias_ref,
    ugain_ref,
    ubias_ref,
    in_sem,
    xs_l,
    save_l,
    save_r,
    left_all,
    right_all,
    left_f,
    right_f,
    dl_recv,
    dr_recv,
    tri_t,
    dtri,
    save_t,
    lsend,
    lrecv,
    rsend,
    rrecv,
    fsend,
    frecv,
    dlsend,
    dlrecv,
    drsend,
    drrecv,
    sibsend,
    sibrecv,
):
    my_ia, my_ja = lax.axis_index("ia"), lax.axis_index("ja")
    rows_i, k_l, ch = slab_ref.shape
    k_r, rows_j, _ = cols_ref.shape

    ins = [
        pltpu.make_async_copy(a, b, in_sem.at[n])
        for n, (a, b) in enumerate(
            [
                (cols_hbm, cols_ref),
                (wr_hbm, wr_ref),
                (gain_hbm, gain_ref),
                (bias_hbm, bias_ref),
                (slab_hbm, slab_ref),
                (wl_hbm, wl_ref),
                (tile_hbm, tile_ref),
                (wg_hbm, wg_ref),
                (cot_hbm, cot_ref),
                (wo_hbm, wo_ref),
                (ugain_hbm, ugain_ref),
                (ubias_hbm, ubias_ref),
            ]
        )
    ]
    for copy in ins:
        copy.start()

    n_z = n_ia // 2
    my_z, my_core = my_ia // 2, lax.rem(my_ia, 2)
    sibling = my_z * 2 + 1 - my_core
    square = n_ja == 4 and k_l % 4 == 0
    quarter = k_l // 4

    def ja_peer(s):
        if square:
            return lax.rem(my_ja // 2 + s // 2, 2) * 2 + lax.rem(my_ja + s, 2)
        return lax.rem(my_ja + s, n_ja)

    def ia_peer(s):
        return lax.rem(my_ia + s, n_ia)

    def z_peer(s):
        return lax.rem(my_z + s, n_z)

    barrier = pltpu.get_barrier_semaphore()

    def greet_ja(s, c):
        pl.semaphore_signal(barrier, inc=1, device_id=(my_ia, ja_peer(s)), device_id_type=MESH)
        return c

    def greet_ia(s, c):
        pl.semaphore_signal(barrier, inc=1, device_id=(ia_peer(s), my_ja), device_id_type=MESH)
        return c

    lax.fori_loop(1, n_ja, greet_ja, 0)
    lax.fori_loop(1, n_ia, greet_ia, 0)

    for copy in ins[:4]:
        copy.wait()
    gain = gain_ref[...]
    bias = bias_ref[...]
    pitch = xs_l.shape[0] // rows_i

    def slab_piece(k0, step):
        return jnp.concatenate(
            [xs_l[pl.ds(k0 + u, rows_i, stride=pitch), :] for u in range(step)], axis=0
        )

    def cols_piece(k0, step):
        return cols_ref[pl.ds(k0, step)].astype(F32).reshape(step * rows_j, ch)

    def project(piece, rows, start, count, w_ref, save, edges, base):
        step = chunk_of(count, rows, 256)

        def body(t, c):
            k0 = start + t * step
            x = piece(k0, step)
            scaled, inverse = normalize(x)
            q = dot((scaled * gain + bias).astype(BF16), w_ref[...])
            linear = q[:, :ch]
            sigma = jax.nn.sigmoid(q[:, ch:])
            at = pl.ds(pl.multiple_of(k0 * rows, 8), step * rows)
            save[0, at, :] = scaled
            save[1, at, :] = jnp.broadcast_to(inverse, scaled.shape)
            save[2, at, :] = linear
            save[3, at, :] = sigma
            edge = (sigma * linear).astype(BF16)
            edges[pl.ds(base + k0, step)] = edge.reshape(step, rows, ch)
            return c

        lax.fori_loop(0, count // step, body, 0)

    def left_copy(s):
        own = left_all.at[pl.ds(my_ja * k_l, k_l)]
        return pltpu.make_async_remote_copy(
            src_ref=own,
            dst_ref=own,
            send_sem=lsend.at[s],
            recv_sem=lrecv.at[s],
            device_id=(my_ia, ja_peer(s)),
            device_id_type=MESH,
        )

    def left_hop(owner, q, to, sem):
        piece = left_all.at[pl.ds(ja_peer(owner) * k_l + q * quarter, quarter)]
        return pltpu.make_async_remote_copy(
            src_ref=piece,
            dst_ref=piece,
            send_sem=lsend.at[sem],
            recv_sem=lrecv.at[sem],
            device_id=(my_ia, ja_peer(to)),
            device_id_type=MESH,
        )

    def own_hop(to, q):
        return left_hop(0, q, to, (to - 1) * 4 + q)

    relays = [left_hop(2 - (q + 1) % 2, q, 2 - q % 2, 8 + q) for q in range(4 * square)]

    def right_copy(s):
        own = right_all.at[pl.ds(my_ia * k_r, k_r)]
        return pltpu.make_async_remote_copy(
            src_ref=own,
            dst_ref=own,
            send_sem=rsend.at[s],
            recv_sem=rrecv.at[s],
            device_id=(z_peer(s) * 2 + my_core, my_ja),
            device_id_type=MESH,
        )

    def right_forward(s):
        piece = right_all.at[pl.ds((z_peer(n_z - s) * 2 + my_core) * k_r, k_r)]
        return pltpu.make_async_remote_copy(
            src_ref=piece,
            dst_ref=piece,
            send_sem=fsend.at[s],
            recv_sem=frecv.at[s],
            device_id=(sibling, my_ja),
            device_id_type=MESH,
        )

    def dl_copy(s):
        to = ja_peer(s)
        return pltpu.make_async_remote_copy(
            src_ref=left_all.at[pl.ds(to * k_l, k_l)],
            dst_ref=dl_recv.at[s],
            send_sem=dlsend.at[s],
            recv_sem=dlrecv.at[s],
            device_id=(my_ia, to),
            device_id_type=MESH,
        )

    def dl_hop(piece, q, to, slot, sem):
        return pltpu.make_async_remote_copy(
            src_ref=left_all.at[pl.ds(ja_peer(piece) * k_l + q * quarter, quarter)],
            dst_ref=dl_recv.at[slot, pl.ds(q * quarter, quarter)],
            send_sem=dlsend.at[sem],
            recv_sem=dlrecv.at[sem],
            device_id=(my_ia, ja_peer(to)),
            device_id_type=MESH,
        )

    def across_hop(q):
        return dl_hop(3, q, 1 + q % 2, 3, q)

    def near_hop(to, q):
        return dl_hop(to, q, to, to, to * 4 + q)

    def dr_sibling(s):
        return pltpu.make_async_remote_copy(
            src_ref=right_all.at[pl.ds((z_peer(s) * 2 + 1 - my_core) * k_r, k_r)],
            dst_ref=dr_recv.at[n_z + s],
            send_sem=sibsend.at[s],
            recv_sem=sibrecv.at[s],
            device_id=(sibling, my_ja),
            device_id_type=MESH,
        )

    def dr_copy(s):
        to = z_peer(s) * 2 + my_core
        return pltpu.make_async_remote_copy(
            src_ref=right_all.at[pl.ds(to * k_r, k_r)],
            dst_ref=dr_recv.at[s],
            send_sem=drsend.at[s],
            recv_sem=drrecv.at[s],
            device_id=(to, my_ja),
            device_id_type=MESH,
        )

    def each(copy, n, act):
        def body(s, c):
            act(copy(s))
            return c

        lax.fori_loop(1, n, body, 0)

    project(cols_piece, rows_j, 0, k_r, wr_ref, save_r, right_all, my_ia * k_r)
    pl.semaphore_wait(barrier, n_ia + n_ja - 2)
    each(right_copy, n_z, lambda c: c.start())
    right_forward(0).start()
    for copy in ins[4:6]:
        copy.wait()

    def widen(r, c):
        xs_l[pl.ds(pl.multiple_of(r * pitch, 8), k_l), :] = slab_ref[r].astype(F32)
        return c

    lax.fori_loop(0, rows_i, widen, 0, unroll=4)
    def project_slab(start, count):
        project(slab_piece, rows_i, start, count, wl_ref, save_l, left_all, my_ja * k_l)

    if square:

        def send_quarter(q, c):
            project_slab(q * quarter, quarter)
            own_hop(1, q).start()
            own_hop(2, q).start()
            return c

        lax.fori_loop(0, 4, send_quarter, 0)
    else:
        project_slab(0, k_l)
        each(left_copy, n_ja, lambda c: c.start())

    def pass_on(s, c):
        right_copy(s).wait_recv()
        right_forward(s).start()
        return c

    def relay(q):
        own_hop(2 - (q + 1) % 2, q).wait_recv()
        relays[q].start()

    if square:
        relay(0)

    for copy in ins[6:]:
        copy.wait()
    ugain = ugain_ref[...]
    ubias = ubias_ref[...]
    t_rows = chunk_of(rows_i, rows_j, 512)
    t_flat = t_rows * rows_j

    def by_j(i):
        return pl.ds(i, rows_j, stride=rows_i)

    def gate_body(t, c):
        x = tile_ref[pl.ds(t * t_rows, t_rows)].astype(F32).reshape(t_flat, ch)
        scaled, inverse = normalize(x)
        gate = jax.nn.sigmoid(dot((scaled * gain + bias).astype(BF16), wg_ref[...]))
        at = pl.ds(pl.multiple_of(t * t_flat, 8), t_flat)
        save_t[0, at, :] = scaled
        save_t[1, at, :] = jnp.broadcast_to(inverse, scaled.shape)
        for u in range(t_rows):
            save_t[2, by_j(t * t_rows + u), :] = gate[u * rows_j : (u + 1) * rows_j]
            save_t[3, by_j(t * t_rows + u), :] = cot_ref[t * t_rows + u].astype(F32)
        return c

    lax.fori_loop(0, rows_i // t_rows, gate_body, 0)

    if square:
        relay(1)
    lax.fori_loop(1, n_z, pass_on, 0)
    if square:
        relay(2)
        relay(3)
    each(right_copy, n_z, lambda c: c.wait_send())
    lax.fori_loop(0, n_z, lambda s, c: (right_forward(s).wait(), c)[1], 0)

    block = math.gcd(rows_j, 8)

    def tri_chunk(s, c):
        if square:

            @pl.when(s == 1)
            def _():
                own_hop(1, 1).wait_recv()
                own_hop(1, 3).wait_recv()

            @pl.when(s == 2)
            def _():
                own_hop(2, 0).wait_recv()
                own_hop(2, 2).wait_recv()

            @pl.when(s == 3)
            def _():
                for copy in relays:
                    copy.wait_recv()

            k_first = ja_peer(s) * k_l
        else:

            @pl.when(s > 0)
            def _():
                left_copy(s).wait()

            k_first = ja_peer(n_ja - s) * k_l

        ks = pl.ds(k_first, k_l)
        left_f[ks] = left_all[ks].astype(F32)
        right_f[ks] = right_all[ks].astype(F32)
        for first in range(0, rows_j, block):

            def tri_body(k, accs, first=first):
                l = left_f[k_first + k]
                return tuple(
                    acc + right_f[k_first + k, pl.ds(first + j, 1), :] * l
                    for j, acc in enumerate(accs)
                )

            accs = tuple(tri_t[pl.ds((first + j) * rows_i, rows_i), :] for j in range(block))
            accs = lax.fori_loop(0, k_l, tri_body, accs, unroll=2)
            for j, acc in enumerate(accs):
                tri_t[pl.ds((first + j) * rows_i, rows_i), :] = acc
        return c

    tri_t[...] = jnp.zeros_like(tri_t)
    lax.fori_loop(0, n_ja, tri_chunk, 0)
    if square:
        for q in range(4):
            own_hop(1, q).wait_send()
            own_hop(2, q).wait_send()
            relays[q].wait_send()

    j_rows = chunk_of(rows_j, rows_i, 512)

    def tile_body(t, c):
        at = pl.ds(pl.multiple_of(t * j_rows * rows_i, 8), j_rows * rows_i)
        scaled, inverse = normalize(tri_t[at, :])
        outer = dot((scaled * ugain + ubias).astype(BF16), wo_ref[...])
        gate, cot = save_t[2, at, :], save_t[3, at, :]
        d_outer = (cot * gate).astype(BF16)
        d_tri = norm_back(scaled, inverse, dot_t(d_outer, wo_ref[...]), ugain)
        tri_t[at, :] = d_tri.astype(BF16).astype(F32)
        update = gate * outer
        save_t[2, at, :] = update
        save_t[3, at, :] = cot * update * (1.0 - gate)
        return c

    lax.fori_loop(0, rows_j // j_rows, tile_body, 0)

    def left_part(s, start=0, count=k_l):
        k_first = ja_peer(s) * k_l + start
        u_l = chunk_of(count, 1, 4)

        def body(t, c):
            k0 = k_first + t * u_l
            accs = [None] * u_l
            for j in range(rows_j):
                d = tri_t[pl.ds(j * rows_i, rows_i), :]
                for u in range(u_l):
                    term = right_f[k0 + u, pl.ds(j, 1), :] * d
                    accs[u] = term if j == 0 else accs[u] + term
            for u in range(u_l):
                left_all[k0 + u] = accs[u].astype(BF16)
            return c

        lax.fori_loop(0, count // u_l, body, 0)

    def right_part(to, came=None):
        k_first = to * k_r
        u_r = math.gcd(k_r, 4)

        def body(t, c):
            k0 = k_first + t * u_r
            accs = [None] * u_r
            for i in range(rows_i):
                d = dtri[pl.ds(i * rows_j, rows_j), :]
                for u in range(u_r):
                    term = left_f[k0 + u, pl.ds(i, 1), :] * d
                    accs[u] = term if i == 0 else accs[u] + term
            for u in range(u_r):
                acc = accs[u]
                if came is not None:
                    acc = acc + dr_recv[came, t * u_r + u].astype(F32)
                right_all[k0 + u] = acc.astype(BF16)
            return c

        lax.fori_loop(0, k_r // u_r, body, 0)

    def for_sibling(v, c):
        s = lax.rem(v + 1, n_z)
        right_part(z_peer(s) * 2 + 1 - my_core)
        dr_sibling(s).start()
        return c

    def for_core(s, c):
        dr_sibling(s).wait_recv()
        right_part(z_peer(s) * 2 + my_core, n_z + s)
        dr_copy(s).start()
        return c

    def for_ja(s, c):
        left_part(s)
        dl_copy(s).start()
        return c

    def across(q, c):
        left_part(3, q * quarter, quarter)
        across_hop(q).start()
        return c

    def add_across(q):
        across_hop(q).wait_recv()
        to = 2 - q % 2
        at = pl.ds(ja_peer(to) * k_l + q * quarter, quarter)
        came = dl_recv[3, pl.ds(q * quarter, quarter)].astype(F32)
        left_all[at] = (left_all[at].astype(F32) + came).astype(BF16)
        near_hop(to, q).start()

    def reorder(i, c):
        dtri[pl.ds(pl.multiple_of(i * rows_j, 8), rows_j), :] = tri_t[by_j(i), :]
        return c

    if square:
        lax.fori_loop(0, 4, across, 0)
        lax.fori_loop(0, rows_i, reorder, 0, unroll=8)
        lax.fori_loop(0, n_z, for_sibling, 0)
        left_part(1)
        near_hop(1, 0).start()
        near_hop(1, 2).start()
        lax.fori_loop(1, n_z, for_core, 0)
        left_part(2)
        near_hop(2, 1).start()
        near_hop(2, 3).start()
        for q in range(4):
            add_across(q)
    else:
        lax.fori_loop(0, rows_i, reorder, 0, unroll=8)
        lax.fori_loop(0, n_z, for_sibling, 0)
        lax.fori_loop(1, n_z, for_core, 0)
        lax.fori_loop(1, n_ja, for_ja, 0)
    left_part(0)
    dr_sibling(0).wait_recv()
    right_part(my_ia)

    def tile_back(t, c):
        at = pl.ds(pl.multiple_of(t * t_flat, 8), t_flat)
        first = t * t_rows
        for u in range(t_rows):
            update_ref[first + u] = save_t[2, by_j(first + u), :].astype(BF16)
        d_gate = jnp.concatenate([save_t[3, by_j(first + u), :] for u in range(t_rows)], axis=0)
        grad = dot_t(d_gate.astype(BF16), wg_ref[...])
        out = norm_back(save_t[0, at, :], save_t[1, at, :], grad, gain)
        gtile_ref[pl.ds(first, t_rows)] = out.astype(BF16).reshape(t_rows, rows_j, ch)
        return c

    lax.fori_loop(0, rows_i // t_rows, tile_back, 0)

    def project_back(put, rows, start, count, w_ref, save, edges, base, recv, first, n):
        step = chunk_of(count, rows, 512)

        def body(t, c):
            k0 = start + t * step
            at = pl.ds(pl.multiple_of(k0 * rows, 8), step * rows)
            d = edges[pl.ds(base + k0, step)].astype(F32)

            def add(s, d):
                return d + recv[s, pl.ds(k0, step)].astype(F32)

            d = lax.fori_loop(first, n, add, d, unroll=n <= 8).reshape(step * rows, ch)
            linear, sigma = save[2, at, :], save[3, at, :]
            p = jnp.concatenate([d * sigma, d * linear * sigma * (1.0 - sigma)], axis=-1)
            grad = dot_t(p.astype(BF16), w_ref[...])
            put(k0, step, norm_back(save[0, at, :], save[1, at, :], grad, gain))
            return c

        lax.fori_loop(0, count // step, body, 0)

    def put_cols(k0, step, out):
        gcols_ref[pl.ds(k0, step)] = out.astype(BF16).reshape(step, rows_j, ch)

    def put_slab(k0, step, out):
        for u in range(step):
            xs_l[pl.ds(k0 + u, rows_i, stride=pitch), :] = out[u * rows_i : (u + 1) * rows_i]

    def back_slab(start, count, last):
        project_back(
            put_slab, rows_i, start, count, wl_ref, save_l, left_all, my_ja * k_l, dl_recv, 1, last
        )

    if square:

        def back_half(h, c):
            for q in (h * 2, h * 2 + 1):
                near_hop(1, q).wait_recv()
                near_hop(2, q).wait_recv()
            back_slab(h * 2 * quarter, 2 * quarter, 3)
            return c

        lax.fori_loop(0, 2, back_half, 0)
        for q in range(4):
            across_hop(q).wait_send()
            near_hop(1, q).wait_send()
            near_hop(2, q).wait_send()
    else:
        each(dl_copy, n_ja, lambda c: c.wait())
        back_slab(0, k_l, n_ja)

    def narrow(r, c):
        gslab_ref[r] = xs_l[pl.ds(pl.multiple_of(r * pitch, 8), k_l), :].astype(BF16)
        return c

    lax.fori_loop(0, rows_i, narrow, 0, unroll=4)

    each(dr_copy, n_z, lambda c: c.wait())
    lax.fori_loop(0, n_z, lambda s, c: (dr_sibling(s).wait_send(), c)[1], 0)
    project_back(
        put_cols, rows_j, 0, k_r, wr_ref, save_r, right_all, my_ia * k_r, dr_recv, 1, n_z + 1
    )


def move(*refs):
    n = len(refs) // 2
    copies = [pltpu.make_async_copy(refs[m], refs[n + m], refs[-1].at[m]) for m in range(n)]
    for copy in copies:
        copy.start()
    for copy in copies:
        copy.wait()


def solution(mesh):
    n_ia, n_ja = mesh.shape["ia"], mesh.shape["ja"]

    def shards(slab, cols, tile, cot, wl, wr, wg, wo, gain, bias, ugain, ubias):
        cols = jnp.transpose(cols, (1, 0, 2))
        rows_i, k_l, ch = slab.shape
        k_r, rows_j, _ = cols.shape
        res = k_l * n_ja
        pitch = -(-k_l // 8) * 8
        anywhere = pl.BlockSpec(memory_space=pl.ANY)
        flat = rows_i * rows_j
        dma = pltpu.SemaphoreType.DMA
        ins = (
            slab, cols, tile, cot, wl, wr, wg, wo,
            gain[None, :], bias[None, :], ugain[None, :], ubias[None, :],
        )
        results = [jax.ShapeDtypeStruct(a.shape, BF16) for a in (tile, slab, cols, tile)]
        buffers = (
            [(a.shape, a.dtype) for a in ins]
            + [
                ((rows_i * pitch, ch), F32),
                ((4, rows_i * k_l, ch), F32),
                ((4, rows_j * k_r, ch), F32),
                ((res, rows_i, ch), BF16),
                ((res, rows_j, ch), BF16),
                ((res, rows_i, ch), F32),
                ((res, rows_j, ch), F32),
                ((n_ja, k_l, rows_i, ch), BF16),
                ((n_ia, k_r, rows_j, ch), BF16),
                ((flat, ch), F32),
                ((flat, ch), F32),
                ((4, flat, ch), F32),
            ]
        )
        scratch = [pltpu.VMEM(shape, kind) for shape, kind in buffers]
        vmem = pl.BlockSpec(memory_space=pltpu.VMEM)
        done = pl.pallas_call(
            functools.partial(kernel, n_ia, n_ja),
            out_shape=[pltpu.VMEM(a.shape, a.dtype) for a in results],
            in_specs=[pl.BlockSpec(memory_space=pltpu.HBM)] * len(ins),
            out_specs=[vmem] * len(results),
            scratch_shapes=scratch[: len(ins)]
            + [dma((len(ins),))]
            + scratch[len(ins) :]
            + [dma((n,)) for n in (n_ja + 8, n_ja + 8, n_ia, n_ia, n_ia, n_ia) * 2],
            compiler_params=pltpu.CompilerParams(
                collective_id=0, has_side_effects=True, vmem_limit_bytes=VMEM_BYTES
            ),
        )(*ins)
        update, gslab, gcols, gtile = pl.pallas_call(
            move,
            out_shape=results,
            in_specs=[vmem] * len(results),
            out_specs=[anywhere] * len(results),
            scratch_shapes=[dma((len(results),))],
            compiler_params=pltpu.CompilerParams(vmem_limit_bytes=VMEM_BYTES),
        )(*[pltpu.with_memory_space_constraint(a, pltpu.VMEM) for a in done])
        return update, gslab, jnp.transpose(gcols, (1, 0, 2)), gtile

    return jax.shard_map(
        shards,
        mesh=mesh,
        in_specs=(
            P("ia", "ja", None),
            P("ja", "ia", None),
            P("ia", "ja", None),
            P("ia", "ja", None),
        )
        + (P(),) * 8,
        out_specs=(
            P("ia", "ja", None),
            P("ia", "ja", None),
            P("ja", "ia", None),
            P("ia", "ja", None),
        ),
        check_vma=False,
    )
```
